32 devices in a mesh: comp: 4 (over z), dom: 8 (over y, x, core).
Axes of the slice: x: 2, y: 2, z: 4, core: 2. Of those that a mesh axis runs over, the one named last changes fastest.
Arguments:
- airside_exchange: bfloat16 [4, 4, 8192], P('comp', None, 'dom'), may hold values from -6 to 6
- regrid_matrix_partitions: bfloat16 [4, 64, 4, 128, 128], P('comp', 'dom'), may hold values from -0.25 to 0.25
- regrid_destination_latitude: int32 [4, 64, 4], P('comp', 'dom'), may hold values from 0 to 255, all different within a row
- thermal_departure: float32 [32, 256, 128], P(None, ('comp', 'dom')), may hold values from -6 to 6
- diffusivity_coefficient: float32 [31, 256, 128], P(None, ('comp', 'dom')), may hold values from 0.05 to 3
- elevation_anomaly_profile: float32 [256, 128], P(('comp', 'dom')), may hold values from -3 to 3
- depth_integrated_volume_flow: float32 [2, 256, 128], P(None, ('comp', 'dom')), may hold values from -2 to 2
- marine_indicator: int32 [256, 128], P(('comp', 'dom')), may hold values 0 or 1
Outputs:
- ocean_temperature: float32 [32, 256, 128], P(None, ('comp', 'dom'))
- ocean_height: float32 [256, 128], P(('comp', 'dom'))
- atm_surface: bfloat16 [4, 2, 8192], P('comp', None, 'dom')
The draws below stay inside these ranges and needn't reach their ends.
Inputs may be any that keep to these rules, and one draw needn't show every extreme that they name: `regrid_destination_latitude`: each (section, source block) names 4 different ocean blocks, and every ocean block is named somewhere; ocean block b is grid row b.
All inputs are finite; a program needn't handle non-finite values. No bound on the sum of `marine_indicator` on one device may be relied on, other than what follows from the above.
Results may differ from the reference program's by a relative error of at most 0.0048.
Values may be sent and summed in bfloat16 or wider, within the bound.
A program may use at most 64 MiB of HBM per device.

```python
import math
import jax
import jax.numpy as jnp
from jax import lax

NF = 4
AC = 1024
BA = 128
MARINE_PATCH_SPAN = 128
K = 4
SB = 8
MARINE_DEPTHS = 32
NSTEP = 2
NSUB = 8
MARINE_LATITUDES = 256
NSRC = 64
N_COMP = 4
N_DOM = 8


def set_ends(entries, rng, least, high):
    spot = [jax.random.randint(jax.random.fold_in(rng, axis), (), 0, length) for axis, length in enumerate(entries.shape)]
    main_axis = entries.shape.index(max(entries.shape))
    beside = spot[:main_axis] + [(spot[main_axis] + 1) % entries.shape[main_axis]] + spot[main_axis + 1:]
    return entries.at[tuple(spot)].set(least).at[tuple(beside)].set(high)


def block_levels(own_key, dims, shards, low, largest):
    level, own = 1.0, jax.random.fold_in(own_key, 6)
    for position, blocks in shards:
        steps = jnp.exp(jax.random.uniform(jax.random.fold_in(own, position), (blocks,), jnp.float32, low / len(shards), largest / len(shards)))
        level = level * jnp.repeat(steps, dims[position] // blocks).reshape([-1 if axis == position else 1 for axis in range(len(dims))])
    return level


def different_ones(rng, rows, number_of, top, lift):
    sequence = jax.random.permutation(jax.random.fold_in(rng, 1), number_of)
    favour = sequence
    for power in range(3):
        favour = favour * favour // number_of
    favour = favour * lift // number_of
    tickets = jax.random.randint(jax.random.fold_in(rng, 2), (rows, number_of), 0, 4096) + favour
    holders = jax.random.permutation(jax.random.fold_in(rng, 3), rows)[jnp.arange(number_of) % rows]
    tickets = jnp.where(jnp.arange(rows)[:, None] == holders[None, :], 1 << 14, tickets)
    score = tickets * number_of + jnp.arange(number_of)
    return lax.top_k(score.astype(jnp.int32), top)[1].astype(jnp.int32)


def gaussian(own_key, extent, width, limit, pieces=(), kind=jnp.bfloat16):
    values = width * jax.random.normal(own_key, extent, jnp.float32)
    if pieces:
        values = values * block_levels(own_key, extent, pieces, -0.22, 0.18)
    return jnp.clip(values, -limit, limit).astype(kind)


def setup_inputs(seed: int = 0) -> dict:
    arg_keys = jax.random.split(jax.random.key(seed), 9)
    return {
        "airside_exchange": gaussian(arg_keys[0], (N_COMP, NF, N_DOM * AC), 1.0, 6.0, ((0, 4), (2, 8))),
        "regrid_matrix_partitions": gaussian(arg_keys[1], (N_COMP, NSRC, K, BA, MARINE_PATCH_SPAN), (4 * BA) ** -0.5, 0.25, ((0, 4), (1, 8))),
        "regrid_destination_latitude": different_ones(arg_keys[2], N_COMP * NSRC, MARINE_LATITUDES, K, 256).reshape((N_COMP, NSRC, K)),
        "thermal_departure": gaussian(arg_keys[3], (MARINE_DEPTHS, MARINE_LATITUDES, MARINE_PATCH_SPAN), 1.0, 6.0, ((1, 32),), jnp.float32),
        "diffusivity_coefficient": jnp.clip(jnp.exp(math.log(3.0) - 4.0943445 * jax.random.uniform(arg_keys[4], (MARINE_DEPTHS - 1, MARINE_LATITUDES, MARINE_PATCH_SPAN), jnp.float32) ** block_levels(arg_keys[4], (MARINE_DEPTHS - 1, MARINE_LATITUDES, MARINE_PATCH_SPAN), ((1, 32),), -0.2, 0.2)), 0.05, 3.0),
        "elevation_anomaly_profile": gaussian(arg_keys[5], (MARINE_LATITUDES, MARINE_PATCH_SPAN), 0.5, 3.0, ((0, 32),), jnp.float32),
        "depth_integrated_volume_flow": gaussian(arg_keys[6], (2, MARINE_LATITUDES, MARINE_PATCH_SPAN), 0.3, 2.0, ((1, 32),), jnp.float32),
        "marine_indicator": set_ends((jax.random.randint(arg_keys[7], (MARINE_LATITUDES, MARINE_PATCH_SPAN), 0, 10) < 7).astype(jnp.int32), jax.random.fold_in(arg_keys[7], 1), 0, 1),
    }


wave_gain = 0.35
stress_gain = 0.1
fresh_gain = 0.1
spread_gain = 0.2
heating_gain = 0.5


def northward(field):
    return jnp.concatenate([field[..., 1:, :], jnp.zeros_like(field[..., :1, :])], axis=-2)


def southward(field):
    return jnp.concatenate([jnp.zeros_like(field[..., :1, :]), field[..., :-1, :]], axis=-2)


def vertical_solve(explicit, diffusivity_coefficient):
    levels_all = explicit.shape[0]
    solved = []
    ratios = []
    for layer_index in range(levels_all):
        upward = diffusivity_coefficient[layer_index - 1] if layer_index > 0 else jnp.zeros_like(explicit[0])
        downward = diffusivity_coefficient[layer_index] if layer_index < levels_all - 1 else jnp.zeros_like(explicit[0])
        pivots = 1.0 + upward + downward
        if layer_index > 0:
            pivots = pivots - upward * ratios[-1]
            solved.append((explicit[layer_index] + upward * solved[-1]) / pivots)
        else:
            solved.append(explicit[layer_index] / pivots)
        ratios.append(downward / pivots)
    result = [solved[-1]]
    for layer_index in range(levels_all - 2, -1, -1):
        result.append(solved[layer_index] + ratios[layer_index] * result[-1])
    return jnp.stack(result[::-1])


def reference(airside_exchange, regrid_matrix_partitions, regrid_destination_latitude, thermal_departure, diffusivity_coefficient, elevation_anomaly_profile, depth_integrated_volume_flow, marine_indicator):
    sources = airside_exchange.astype(jnp.float32).reshape(N_COMP, NF, N_DOM * SB, BA)
    weights = regrid_matrix_partitions.astype(jnp.float32)
    partial_terms = jnp.einsum("cfra,crkab->crkfb", sources, weights)
    ocean_flux = jnp.zeros((MARINE_LATITUDES, NF, MARINE_PATCH_SPAN), jnp.float32).at[regrid_destination_latitude.reshape(-1)].add(partial_terms.reshape(-1, NF, MARINE_PATCH_SPAN))
    heating = ocean_flux[:, 0, :]
    freshwater = ocean_flux[:, 1, :]
    stress_east = ocean_flux[:, 2, :]
    stress_north = ocean_flux[:, 3, :]
    wet = marine_indicator.astype(jnp.float32)
    face_east = wet * jnp.roll(wet, -1, axis=1)
    face_north = wet * northward(wet)
    height = elevation_anomaly_profile
    flow_east = depth_integrated_volume_flow[0]
    flow_north = depth_integrated_volume_flow[1]
    advected_quantity = thermal_departure
    for outer_step in range(NSTEP):
        for substep in range(NSUB):
            new_east = face_east * (flow_east - wave_gain * (jnp.roll(height, -1, axis=1) - height) + stress_gain * stress_east)
            new_north = face_north * (flow_north - wave_gain * (northward(height) - height) + stress_gain * stress_north)
            height = height - wave_gain * (new_east - jnp.roll(new_east, 1, axis=1) + new_north - southward(new_north)) + fresh_gain * freshwater * wet
            flow_east = new_east
            flow_north = new_north
        along_east = face_east * (jnp.roll(advected_quantity, -1, axis=2) - advected_quantity)
        along_north = face_north * (northward(advected_quantity) - advected_quantity)
        laplace = along_east - jnp.roll(along_east, 1, axis=2) + along_north - southward(along_north)
        explicit = advected_quantity + spread_gain * laplace
        explicit = explicit.at[0].add(heating_gain * heating * wet)
        advected_quantity = vertical_solve(explicit, diffusivity_coefficient)
    surface = jnp.stack([advected_quantity[0], height]).astype(jnp.bfloat16)
    surface = lax.optimization_barrier(surface)
    picked = surface[:, regrid_destination_latitude, :].astype(jnp.float32)
    returned = jnp.einsum("fcrkb,crkab->cfra", picked, weights)
    return advected_quantity, height, returned.reshape(N_COMP, 2, N_DOM * AC).astype(jnp.bfloat16)
```

```python
import functools

import jax
import jax.numpy as jnp
from jax import lax
from jax.experimental import pallas as pl
from jax.experimental.pallas import tpu as pltpu
from jax.sharding import PartitionSpec as P

NSTEP = 2
NSUB = 8

wave_gain = 0.35
stress_gain = 0.1
fresh_gain = 0.1
spread_gain = 0.2
heating_gain = 0.5

MESH = pl.DeviceIdType.MESH
F32 = jnp.float32
BF16 = jnp.bfloat16


def idiv(value, by):
    if by & (by - 1) == 0:
        return lax.shift_right_logical(value, jnp.full_like(value, by.bit_length() - 1))
    return value // by


def imod(value, by):
    if by & (by - 1) == 0:
        return value & (by - 1)
    return value % by


def wrapped(value, count):
    value = jnp.where(value >= count, value - count, value)
    return jnp.where(value < 0, value + count, value)


def iota(shape, dim):
    return lax.broadcasted_iota(jnp.int32, shape, dim)


def east(v):
    return pltpu.roll(v, v.shape[-1] - 1, v.ndim - 1)


def west(v):
    return pltpu.roll(v, 1, v.ndim - 1)


def north(v):
    return pltpu.roll(v, v.shape[-2] - 1, v.ndim - 2)


def south(v):
    return pltpu.roll(v, 1, v.ndim - 2)


def kernel(
    count,
    blocks_dom,
    air_ref,
    weight_ref,
    target_ref,
    tracer_ref,
    mix_ref,
    height_ref,
    flow_ref,
    wet_ref,
    out_tracer,
    out_height,
    out_air,
    terms,
    dense,
    flux_in,
    base_out,
    base_in,
    edge_out,
    edge_in,
    force_out,
    force_in,
    second_out,
    second_in,
    surface_all,
    inverse,
    carry,
    ratio,
    response,
    work,
    flux_sems,
    base_send,
    base_recv,
    edge_send,
    edge_recv,
    force_send,
    force_recv,
    second_send,
    second_recv,
    surface_sems,
):
    group, block = lax.axis_index("comp"), lax.axis_index("dom")
    me = group * blocks_dom + block
    fields = air_ref.shape[1]
    sources, links, cols, width = weight_ref.shape[1:]
    levels, rows = tracer_ref.shape[:2]
    steps = NSTEP * NSUB
    reach = -(-steps // rows)
    offsets = [d for d in range(-reach, reach + 1) if d != 0]
    pair = 2 if sources % 2 == 0 else 1

    def device(offset):
        peer = lax.rem(me + offset + count, count)
        return (peer // blocks_dom, lax.rem(peer, blocks_dom))

    def copy_to(offset, src, dst, send, recv):
        return pltpu.make_async_remote_copy(
            src_ref=src,
            dst_ref=dst,
            send_sem=send,
            recv_sem=recv,
            device_id=device(offset),
            device_id_type=MESH,
        )

    barrier = pltpu.get_barrier_semaphore()

    def greet(offset, _):
        pl.semaphore_signal(barrier, inc=1, device_id=device(offset), device_id_type=MESH)
        return 0

    lax.fori_loop(1, count, greet, 0)

    wet = wet_ref[...].astype(F32)
    base_out[pl.ds(0, rows), :] = height_ref[...]
    base_out[pl.ds(rows, rows), :] = flow_ref[0]
    base_out[pl.ds(2 * rows, rows), :] = flow_ref[1]
    base_out[pl.ds(3 * rows, rows), :] = wet
    edge_out[0, pl.ds(0, levels), :] = tracer_ref[:, rows - 1, :]
    edge_out[1, pl.ds(0, levels), :] = tracer_ref[:, 0, :]
    edge_out[0, pl.ds(levels, rows), :] = wet
    edge_out[1, pl.ds(levels, rows), :] = wet

    exchange = air_ref[0].astype(F32)
    group_rows = pair * fields
    own = idiv(iota((group_rows, pair * cols), 0), fields) == idiv(
        iota((group_rows, pair * cols), 1), cols
    )
    for p in range(sources // pair):
        part = exchange[:, p * pair * cols : (p + 1) * pair * cols]
        lhs = jnp.where(own, jnp.concatenate([part] * pair, axis=0), 0.0).astype(BF16)
        for k in range(links):
            rhs = weight_ref[0, pl.ds(p * pair, pair), k].reshape(pair * cols, width)
            terms[pl.ds((p * links + k) * group_rows, group_rows), :] = jnp.dot(
                lhs, rhs, preferred_element_type=F32
            )
    every = sources * links * fields
    target = target_ref[0]
    lane = iota((sources, every), 1)
    lane_field = imod(lane, fields)
    lane_source = idiv(lane, group_rows * links) * pair + imod(idiv(lane, fields), pair)
    lane_link = imod(idiv(lane, group_rows), links)
    here = lane_source == iota((sources, every), 0)
    lane_target = jnp.zeros((sources, every), jnp.int32)
    for k in range(links):
        lane_target = jnp.where(here & (lane_link == k), target[:, k : k + 1], lane_target)
    lane_target = jnp.sum(lane_target, axis=0, keepdims=True)
    lane_key = lane_target * fields + lane_field[:1]
    value = terms[...]
    upper = value.astype(BF16)
    lower = (value - upper.astype(F32)).astype(BF16)
    split = jnp.concatenate([upper, lower], axis=0)

    pl.semaphore_wait(barrier, count - 1)

    edges = [
        copy_to(1, edge_out.at[0], edge_in.at[0], edge_send.at[0], edge_recv.at[0]),
        copy_to(-1, edge_out.at[1], edge_in.at[1], edge_send.at[1], edge_recv.at[1]),
    ]
    for copy in edges:
        copy.start()

    chunk = 8 if count % 8 == 0 else 1
    shape = (chunk, fields, rows, every)

    def place(c, _):
        slot = iota(shape, 0) + c * chunk
        row_key = (wrapped(slot + me, count) * rows + iota(shape, 2)) * fields + iota(shape, 1)
        row_key = row_key.reshape(chunk * fields * rows, every)
        hot = jnp.where(row_key == lane_key, 1.0, 0.0).astype(BF16)
        hot = jnp.concatenate([hot, hot], axis=1)
        placed = jnp.dot(hot, split, preferred_element_type=F32)
        dense[pl.ds(c * chunk, chunk)] = placed.astype(BF16).reshape(
            chunk, fields * rows, width
        )

        def send(b, _):
            slot = c * chunk + b

            @pl.when(slot > 0)
            def _():
                copy_to(
                    slot, dense.at[slot], flux_in.at[slot], flux_sems.at[0], flux_sems.at[1]
                ).start()

            return 0

        lax.fori_loop(0, chunk, send, 0)
        return 0

    lax.fori_loop(0, count // chunk, place, 0)

    bases = []
    for i, offset in enumerate(offsets):
        arrives = offsets.index(-offset)
        bases.append(
            copy_to(offset, base_out, base_in.at[arrives], base_send.at[i], base_recv.at[arrives])
        )
    for copy in bases:
        copy.start()

    zero = jnp.zeros((rows, width), F32)
    last_ratio = None
    last_response = None
    for l in range(levels):
        up = mix_ref[l - 1] if l > 0 else zero
        down = mix_ref[l] if l < levels - 1 else zero
        pivot = 1.0 + up + down
        if l > 0:
            pivot = pivot - up * last_ratio
        inv = 1.0 / pivot
        inverse[l] = inv
        carry[l] = up * inv
        last_response = inv if l == 0 else up * inv * last_response
        response[l] = last_response
        last_ratio = down * inv
        ratio[l] = last_ratio
    for l in range(levels - 2, -1, -1):
        last_response = response[l] + ratio[l] * last_response
        response[l] = last_response

    for copy in edges:
        copy.wait_recv()
    row = iota((rows, width), 0)
    top = row == rows - 1
    bottom = row == 0
    wet_north = jnp.where(top, edge_in[1, pl.ds(levels, 1), :], north(wet))
    wet_south = jnp.where(bottom, edge_in[0, pl.ds(levels + rows - 1, 1), :], south(wet))
    inside_top = jnp.logical_not(top & (me == count - 1))
    inside_bottom = jnp.logical_not(bottom & (me == 0))
    mix_east = spread_gain * wet * east(wet)
    mix_west = spread_gain * wet * west(wet)
    mix_north = jnp.where(inside_top, spread_gain * wet * wet_north, 0.0)
    mix_south = jnp.where(inside_bottom, spread_gain * wet * wet_south, 0.0)
    mix_own = 1.0 - (mix_east + mix_west + mix_north + mix_south)

    def solve(source, halo, result, gain):
        swept = None
        for l in range(levels):
            v = source[l]
            v_north = jnp.where(top, halo[1, pl.ds(l, 1), :], north(v))
            v_south = jnp.where(bottom, halo[0, pl.ds(l, 1), :], south(v))
            explicit = (
                mix_own * v
                + mix_east * east(v)
                + mix_west * west(v)
                + mix_north * v_north
                + mix_south * v_south
            )
            if l == 0 and gain is not None:
                explicit = explicit + gain
            swept = explicit * inverse[l] if l == 0 else explicit * inverse[l] + carry[l] * swept
            result[l] = swept
        for l in range(levels - 2, -1, -1):
            swept = result[l] + ratio[l] * swept
            result[l] = swept

    solve(tracer_ref, edge_in, work, None)

    whole = copy_to(
        1,
        dense.at[pl.ds(1, count - 1)],
        flux_in.at[pl.ds(1, count - 1)],
        flux_sems.at[0],
        flux_sems.at[1],
    )
    whole.wait_recv()

    flux = lax.fori_loop(
        1, count, lambda j, total: total + flux_in[j].astype(F32), dense[0].astype(F32)
    )
    heating = flux[0:rows]
    fresh = flux[rows : 2 * rows]
    force_out[pl.ds(0, rows), :] = fresh * wet
    force_out[pl.ds(rows, 2 * rows), :] = flux[2 * rows : 4 * rows]
    forces = []
    for i, offset in enumerate(offsets):
        arrives = offsets.index(-offset)
        forces.append(
            copy_to(
                offset, force_out, force_in.at[arrives], force_send.at[i], force_recv.at[arrives]
            )
        )
    for copy in forces:
        copy.start()

    heat = heating_gain * heating * wet
    for l in range(levels):
        work[l] = work[l] + heat * response[l]
    second_out[0] = work[:, rows - 1, :]
    second_out[1] = work[:, 0, :]
    seconds = [
        copy_to(1, second_out.at[0], second_in.at[0], second_send.at[0], second_recv.at[0]),
        copy_to(-1, second_out.at[1], second_in.at[1], second_send.at[1], second_recv.at[1]),
    ]
    for copy in seconds:
        copy.start()

    for copy in bases:
        copy.wait_recv()

    def window(own_ref, arrived, start):
        parts = []
        for offset in range(-reach, reach + 1):
            if offset == 0:
                parts.append(own_ref[pl.ds(start, rows), :])
            else:
                parts.append(arrived[offsets.index(offset), pl.ds(start, rows), :])
        return jnp.concatenate(parts, axis=0)

    tall = (2 * reach + 1) * rows
    height = window(base_out, base_in, 0)
    flow_east = window(base_out, base_in, rows)
    flow_north = window(base_out, base_in, 2 * rows)
    wet_tall = window(base_out, base_in, 3 * rows)
    number = wrapped(me * rows - reach * rows + iota((tall, width), 0), count * rows)
    face_east = wet_tall * east(wet_tall)
    face_north = jnp.where(number == count * rows - 1, 0.0, wet_tall * north(wet_tall))
    face_west = west(face_east)
    face_south = south(face_north)
    square = wave_gain * wave_gain
    gain_east = square * face_east
    gain_west = square * face_west
    gain_north = square * face_north
    gain_south = square * face_south
    gain_own = gain_east + gain_west + gain_north + gain_south
    flow_east = wave_gain * face_east * flow_east
    flow_north = wave_gain * face_north * flow_north
    spread = flow_east - west(flow_east) + flow_north - south(flow_north)

    for copy in forces:
        copy.wait_recv()
    fresh_tall = fresh_gain * window(force_out, force_in, 0)
    push_east = (wave_gain * stress_gain) * face_east * window(force_out, force_in, rows)
    push_north = (wave_gain * stress_gain) * face_north * window(force_out, force_in, 2 * rows)
    push = push_east - west(push_east) + push_north - south(push_north)

    left = steps
    for stage in range(reach):
        turns = min(rows, left)
        left -= turns

        def subcycle(_, state):
            height, spread = state
            spread = (
                spread
                + push
                + gain_own * height
                - gain_east * east(height)
                - gain_west * west(height)
                - gain_north * north(height)
                - gain_south * south(height)
            )
            return height - spread + fresh_tall, spread

        height, spread = lax.fori_loop(0, turns, subcycle, (height, spread))
        trim = lambda v: v[rows:-rows]
        height, spread, push, fresh_tall = map(trim, (height, spread, push, fresh_tall))
        gain_own, gain_east, gain_west, gain_north, gain_south = map(
            trim, (gain_own, gain_east, gain_west, gain_north, gain_south)
        )
    out_height[...] = height

    for copy in seconds:
        copy.wait_recv()
    solve(work, second_in, out_tracer, heat)

    surface_all[0] = jnp.concatenate([out_tracer[0], height], axis=0).astype(BF16)

    def share(slot, _):
        copy_to(
            slot, surface_all.at[0], surface_all.at[slot], surface_sems.at[0], surface_sems.at[1]
        ).start()
        return 0

    lax.fori_loop(1, count, share, 0)

    high = 2 * rows
    spot = iota((sources, count * high), 1)
    spot_row = wrapped(me - idiv(spot, high), count) * rows + imod(spot, rows)
    spot_field = idiv(imod(spot, high), rows)
    picks = []
    for k in range(links):
        match = spot_row == target[:, k : k + 1]
        for f in range(2):
            picks.append(jnp.where(match & (spot_field == f), 1.0, 0.0))
    picks = jnp.concatenate(picks, axis=0).astype(BF16)

    everyone = copy_to(
        1,
        surface_all.at[pl.ds(1, count - 1)],
        surface_all.at[pl.ds(1, count - 1)],
        surface_sems.at[0],
        surface_sems.at[1],
    )
    everyone.wait_recv()
    chosen = jnp.dot(
        picks, surface_all[...].reshape(count * high, width), preferred_element_type=F32
    ).astype(BF16)
    both = 2 * sources
    chosen = jnp.concatenate([chosen[k * both : (k + 1) * both] for k in range(links)], axis=1)
    results = []
    for p in range(sources // pair):
        rhs = jnp.concatenate(
            [
                weight_ref[0, pl.ds(p * pair, pair), k].reshape(pair * cols, width)
                for k in range(links)
            ],
            axis=1,
        )
        full = lax.dot_general(
            chosen, rhs, (((1,), (1,)), ((), ())), preferred_element_type=F32
        ).reshape(2, sources, pair * cols)
        belongs = iota(full.shape, 1) == p * pair + idiv(iota(full.shape, 2), cols)
        results.append(jnp.sum(jnp.where(belongs, full, 0.0), axis=1))
    out_air[0] = jnp.concatenate(results, axis=1).astype(BF16)

    for copy in edges + bases + forces + seconds:
        copy.wait_send()
    whole.wait_send()
    everyone.wait_send()


def shards(count, blocks_dom, air, weights, targets, tracer, mix, height, flow, wet):
    fields = air.shape[1]
    sources, links = weights.shape[1:3]
    levels, rows, width = tracer.shape
    sides = 2 * -(-NSTEP * NSUB // rows)
    column = pltpu.VMEM((levels, rows, width), F32)
    spec = pl.BlockSpec(memory_space=pltpu.VMEM)
    dma = pltpu.SemaphoreType.DMA
    return pl.pallas_call(
        functools.partial(kernel, count, blocks_dom),
        out_shape=(
            jax.ShapeDtypeStruct(tracer.shape, F32),
            jax.ShapeDtypeStruct(height.shape, F32),
            jax.ShapeDtypeStruct((1, 2, air.shape[2]), BF16),
        ),
        in_specs=[spec] * 8,
        out_specs=(spec,) * 3,
        scratch_shapes=[
            pltpu.VMEM((sources * links * fields, width), F32),
            pltpu.VMEM((count, fields * rows, width), BF16),
            pltpu.VMEM((count, fields * rows, width), BF16),
            pltpu.VMEM((4 * rows, width), F32),
            pltpu.VMEM((sides, 4 * rows, width), F32),
            pltpu.VMEM((2, levels + rows, width), F32),
            pltpu.VMEM((2, levels + rows, width), F32),
            pltpu.VMEM((3 * rows, width), F32),
            pltpu.VMEM((sides, 3 * rows, width), F32),
            pltpu.VMEM((2, levels, width), F32),
            pltpu.VMEM((2, levels, width), F32),
            pltpu.VMEM((count, 2 * rows, width), BF16),
            column,
            column,
            column,
            column,
            column,
            dma((2,)),
            dma((sides,)),
            dma((sides,)),
            dma((2,)),
            dma((2,)),
            dma((sides,)),
            dma((sides,)),
            dma((2,)),
            dma((2,)),
            dma((2,)),
        ],
        compiler_params=pltpu.CompilerParams(
            collective_id=0, has_side_effects=True, vmem_limit_bytes=32 * 1024 * 1024
        ),
    )(air, weights, targets, tracer, mix, height, flow, wet)


def solution(mesh):
    count = mesh.shape["comp"] * mesh.shape["dom"]
    return jax.shard_map(
        functools.partial(shards, count, mesh.shape["dom"]),
        mesh=mesh,
        in_specs=(
            P("comp", None, "dom"),
            P("comp", "dom", None, None, None),
            P("comp", "dom", None),
            P(None, ("comp", "dom"), None),
            P(None, ("comp", "dom"), None),
            P(("comp", "dom"), None),
            P(None, ("comp", "dom"), None),
            P(("comp", "dom"), None),
        ),
        out_specs=(
            P(None, ("comp", "dom"), None),
            P(("comp", "dom"), None),
            P("comp", None, "dom"),
        ),
        check_vma=False,
    )
```

```python
import functools

import jax
import jax.numpy as jnp
from jax import lax
from jax.experimental import pallas as pl
from jax.experimental.pallas import tpu as pltpu
from jax.sharding import PartitionSpec as P

NSTEP = 2
NSUB = 8

wave_gain = 0.35
stress_gain = 0.1
fresh_gain = 0.1
spread_gain = 0.2
heating_gain = 0.5

MESH = pl.DeviceIdType.MESH
F32 = jnp.float32
BF16 = jnp.bfloat16


def idiv(value, by):
    if by & (by - 1) == 0:
        return lax.shift_right_logical(value, jnp.full_like(value, by.bit_length() - 1))
    return value // by


def imod(value, by):
    if by & (by - 1) == 0:
        return value & (by - 1)
    return value % by


def wrapped(value, count):
    value = jnp.where(value >= count, value - count, value)
    return jnp.where(value < 0, value + count, value)


def iota(shape, dim):
    return lax.broadcasted_iota(jnp.int32, shape, dim)


def east(v):
    return pltpu.roll(v, v.shape[-1] - 1, v.ndim - 1)


def west(v):
    return pltpu.roll(v, 1, v.ndim - 1)


def north(v):
    return pltpu.roll(v, v.shape[-2] - 1, v.ndim - 2)


def south(v):
    return pltpu.roll(v, 1, v.ndim - 2)


def kernel(
    count,
    blocks_dom,
    air_hbm,
    weight_hbm,
    target_hbm,
    tracer_hbm,
    mix_hbm,
    height_hbm,
    flow_hbm,
    wet_hbm,
    out_tracer,
    out_height,
    weight_ref,
    surface_all,
    out_picks,
    air_ref,
    target_ref,
    tracer_ref,
    mix_ref,
    wet_ref,
    terms,
    dense,
    flux_in,
    base_out,
    base_in,
    edge_out,
    edge_in,
    force_out,
    force_in,
    second_out,
    second_in,
    inverse,
    carry,
    ratio,
    response,
    work,
    load_sems,
    weight_sems,
    flux_sems,
    base_send,
    base_recv,
    edge_send,
    edge_recv,
    force_send,
    force_recv,
    second_send,
    second_recv,
    surface_sems,
):
    group, block = lax.axis_index("comp"), lax.axis_index("dom")
    me = group * blocks_dom + block
    fields = air_ref.shape[1]
    sources, links, cols, width = weight_ref.shape[1:]
    levels, rows = tracer_ref.shape[:2]
    steps = NSTEP * NSUB
    reach = -(-steps // rows)
    offsets = [d for d in range(-reach, reach + 1) if d != 0]
    pair = 2 if sources % 2 == 0 else 1

    def device(offset):
        peer = lax.rem(me + offset + count, count)
        return (peer // blocks_dom, lax.rem(peer, blocks_dom))

    def copy_to(offset, src, dst, send, recv):
        return pltpu.make_async_remote_copy(
            src_ref=src,
            dst_ref=dst,
            send_sem=send,
            recv_sem=recv,
            device_id=device(offset),
            device_id_type=MESH,
        )

    pairs = sources // pair
    weight_loads = [
        pltpu.make_async_copy(
            weight_hbm.at[:, pl.ds(p * pair, pair)],
            weight_ref.at[:, pl.ds(p * pair, pair)],
            weight_sems.at[p],
        )
        for p in range(pairs)
    ]
    loads = [
        pltpu.make_async_copy(src, dst, load_sems.at[i])
        for i, (src, dst) in enumerate(
            [
                (air_hbm, air_ref),
                (target_hbm, target_ref),
                (wet_hbm, wet_ref),
                (tracer_hbm, tracer_ref),
                (height_hbm, base_out.at[pl.ds(0, rows)]),
                (flow_hbm.at[0], base_out.at[pl.ds(rows, rows)]),
                (flow_hbm.at[1], base_out.at[pl.ds(2 * rows, rows)]),
                (mix_hbm, mix_ref),
            ]
        )
    ]
    for copy in loads[:2] + weight_loads + loads[2:]:
        copy.start()

    barrier = pltpu.get_barrier_semaphore()

    def greet(offset, _):
        pl.semaphore_signal(barrier, inc=1, device_id=device(offset), device_id_type=MESH)
        return 0

    lax.fori_loop(1, count, greet, 0)

    loads[0].wait()
    loads[1].wait()
    exchange = air_ref[0].astype(F32)
    group_rows = pair * fields
    own = idiv(iota((group_rows, pair * cols), 0), fields) == idiv(
        iota((group_rows, pair * cols), 1), cols
    )
    for p in range(pairs):
        weight_loads[p].wait()
        part = exchange[:, p * pair * cols : (p + 1) * pair * cols]
        lhs = jnp.where(own, jnp.concatenate([part] * pair, axis=0), 0.0).astype(BF16)
        for k in range(links):
            rhs = weight_ref[0, pl.ds(p * pair, pair), k].reshape(pair * cols, width)
            terms[pl.ds((p * links + k) * group_rows, group_rows), :] = jnp.dot(
                lhs, rhs, preferred_element_type=F32
            )
    every = sources * links * fields
    diagonal = iota((sources, sources), 0) == iota((sources, sources), 1)
    numbers = target_ref[0].astype(F32)
    target = [
        jnp.sum(jnp.where(diagonal, numbers[k : k + 1], 0.0), axis=1, keepdims=True).astype(
            jnp.int32
        )
        for k in range(links)
    ]
    lane = iota((sources, every), 1)
    lane_field = imod(lane, fields)
    lane_source = idiv(lane, group_rows * links) * pair + imod(idiv(lane, fields), pair)
    lane_link = imod(idiv(lane, group_rows), links)
    here = lane_source == iota((sources, every), 0)
    lane_target = jnp.zeros((sources, every), jnp.int32)
    for k in range(links):
        lane_target = jnp.where(here & (lane_link == k), target[k], lane_target)
    lane_target = jnp.sum(lane_target, axis=0, keepdims=True)
    lane_key = lane_target * fields + lane_field[:1]
    value = terms[...]
    upper = value.astype(BF16)
    lower = (value - upper.astype(F32)).astype(BF16)
    split = jnp.concatenate([upper, lower], axis=0)

    for copy in loads[2:4]:
        copy.wait()
    wet = wet_ref[...].astype(F32)
    base_out[pl.ds(3 * rows, rows), :] = wet
    edge_out[0, pl.ds(0, levels), :] = tracer_ref[:, rows - 1, :]
    edge_out[1, pl.ds(0, levels), :] = tracer_ref[:, 0, :]
    edge_out[0, pl.ds(levels, rows), :] = wet
    edge_out[1, pl.ds(levels, rows), :] = wet

    pl.semaphore_wait(barrier, count - 1)

    edges = [
        copy_to(1, edge_out.at[0], edge_in.at[0], edge_send.at[0], edge_recv.at[0]),
        copy_to(-1, edge_out.at[1], edge_in.at[1], edge_send.at[1], edge_recv.at[1]),
    ]
    for copy in edges:
        copy.start()

    chunk = 8 if count % 8 == 0 else 1
    shape = (chunk, fields, rows, every)

    def place(c, _):
        slot = iota(shape, 0) + c * chunk
        row_key = (wrapped(slot + me, count) * rows + iota(shape, 2)) * fields + iota(shape, 1)
        row_key = row_key.reshape(chunk * fields * rows, every)
        hot = jnp.where(row_key == lane_key, 1.0, 0.0).astype(BF16)
        hot = jnp.concatenate([hot, hot], axis=1)
        placed = jnp.dot(hot, split, preferred_element_type=F32)
        dense[pl.ds(c * chunk, chunk)] = placed.astype(BF16).reshape(
            chunk, fields * rows, width
        )

        def send(b, _):
            slot = c * chunk + b

            @pl.when(slot > 0)
            def _():
                copy_to(
                    slot, dense.at[slot], flux_in.at[slot], flux_sems.at[0], flux_sems.at[1]
                ).start()

            return 0

        lax.fori_loop(0, chunk, send, 0)
        return 0

    lax.fori_loop(0, count // chunk, place, 0)

    for copy in loads[4:]:
        copy.wait()
    bases = []
    for i, offset in enumerate(offsets):
        arrives = offsets.index(-offset)
        bases.append(
            copy_to(offset, base_out, base_in.at[arrives], base_send.at[i], base_recv.at[arrives])
        )
    for copy in bases:
        copy.start()

    zero = jnp.zeros((rows, width), F32)
    last_ratio = None
    last_response = None
    for l in range(levels):
        up = mix_ref[l - 1] if l > 0 else zero
        down = mix_ref[l] if l < levels - 1 else zero
        pivot = 1.0 + up + down
        if l > 0:
            pivot = pivot - up * last_ratio
        inv = 1.0 / pivot
        inverse[l] = inv
        carry[l] = up * inv
        last_response = inv if l == 0 else up * inv * last_response
        response[l] = last_response
        last_ratio = down * inv
        ratio[l] = last_ratio
    for l in range(levels - 2, -1, -1):
        last_response = response[l] + ratio[l] * last_response
        response[l] = last_response

    for copy in edges:
        copy.wait_recv()
    row = iota((rows, width), 0)
    top = row == rows - 1
    bottom = row == 0
    wet_north = jnp.where(top, edge_in[1, pl.ds(levels, 1), :], north(wet))
    wet_south = jnp.where(bottom, edge_in[0, pl.ds(levels + rows - 1, 1), :], south(wet))
    inside_top = jnp.logical_not(top & (me == count - 1))
    inside_bottom = jnp.logical_not(bottom & (me == 0))
    mix_east = spread_gain * wet * east(wet)
    mix_west = spread_gain * wet * west(wet)
    mix_north = jnp.where(inside_top, spread_gain * wet * wet_north, 0.0)
    mix_south = jnp.where(inside_bottom, spread_gain * wet * wet_south, 0.0)
    mix_own = 1.0 - (mix_east + mix_west + mix_north + mix_south)

    def solve(source, halo, result, gain):
        swept = None
        for l in range(levels):
            v = source[l]
            v_north = jnp.where(top, halo[1, pl.ds(l, 1), :], north(v))
            v_south = jnp.where(bottom, halo[0, pl.ds(l, 1), :], south(v))
            explicit = (
                mix_own * v
                + mix_east * east(v)
                + mix_west * west(v)
                + mix_north * v_north
                + mix_south * v_south
            )
            if l == 0 and gain is not None:
                explicit = explicit + gain
            swept = explicit * inverse[l] if l == 0 else explicit * inverse[l] + carry[l] * swept
            result[l] = swept
        for l in range(levels - 2, -1, -1):
            swept = result[l] + ratio[l] * swept
            result[l] = swept

    solve(tracer_ref, edge_in, work, None)

    whole = copy_to(
        1,
        dense.at[pl.ds(1, count - 1)],
        flux_in.at[pl.ds(1, count - 1)],
        flux_sems.at[0],
        flux_sems.at[1],
    )
    whole.wait_recv()

    flux = lax.fori_loop(
        1, count, lambda j, total: total + flux_in[j].astype(F32), dense[0].astype(F32)
    )
    heating = flux[0:rows]
    fresh = flux[rows : 2 * rows]
    force_out[pl.ds(0, rows), :] = fresh * wet
    force_out[pl.ds(rows, 2 * rows), :] = flux[2 * rows : 4 * rows]
    forces = []
    for i, offset in enumerate(offsets):
        arrives = offsets.index(-offset)
        forces.append(
            copy_to(
                offset, force_out, force_in.at[arrives], force_send.at[i], force_recv.at[arrives]
            )
        )
    for copy in forces:
        copy.start()

    heat = heating_gain * heating * wet
    for l in range(levels):
        work[l] = work[l] + heat * response[l]
    second_out[0] = work[:, rows - 1, :]
    second_out[1] = work[:, 0, :]
    seconds = [
        copy_to(1, second_out.at[0], second_in.at[0], second_send.at[0], second_recv.at[0]),
        copy_to(-1, second_out.at[1], second_in.at[1], second_send.at[1], second_recv.at[1]),
    ]
    for copy in seconds:
        copy.start()

    for copy in bases:
        copy.wait_recv()

    def window(own_ref, arrived, start):
        parts = []
        for offset in range(-reach, reach + 1):
            if offset == 0:
                parts.append(own_ref[pl.ds(start, rows), :])
            else:
                parts.append(arrived[offsets.index(offset), pl.ds(start, rows), :])
        return jnp.concatenate(parts, axis=0)

    tall = (2 * reach + 1) * rows
    height = window(base_out, base_in, 0)
    flow_east = window(base_out, base_in, rows)
    flow_north = window(base_out, base_in, 2 * rows)
    wet_tall = window(base_out, base_in, 3 * rows)
    number = wrapped(me * rows - reach * rows + iota((tall, width), 0), count * rows)
    face_east = wet_tall * east(wet_tall)
    face_north = jnp.where(number == count * rows - 1, 0.0, wet_tall * north(wet_tall))
    face_west = west(face_east)
    face_south = south(face_north)
    square = wave_gain * wave_gain
    gain_east = square * face_east
    gain_west = square * face_west
    gain_north = square * face_north
    gain_south = square * face_south
    gain_own = gain_east + gain_west + gain_north + gain_south
    flow_east = wave_gain * face_east * flow_east
    flow_north = wave_gain * face_north * flow_north
    spread = flow_east - west(flow_east) + flow_north - south(flow_north)

    for copy in forces:
        copy.wait_recv()
    fresh_tall = fresh_gain * window(force_out, force_in, 0)
    push_east = (wave_gain * stress_gain) * face_east * window(force_out, force_in, rows)
    push_north = (wave_gain * stress_gain) * face_north * window(force_out, force_in, 2 * rows)
    push = push_east - west(push_east) + push_north - south(push_north)

    left = steps
    for stage in range(reach):
        turns = min(rows, left)
        left -= turns

        def subcycle(_, state):
            height, spread = state
            spread = (
                spread
                + push
                + gain_own * height
                - gain_east * east(height)
                - gain_west * west(height)
                - gain_north * north(height)
                - gain_south * south(height)
            )
            return height - spread + fresh_tall, spread

        height, spread = lax.fori_loop(0, turns, subcycle, (height, spread))
        trim = lambda v: v[rows:-rows]
        height, spread, push, fresh_tall = map(trim, (height, spread, push, fresh_tall))
        gain_own, gain_east, gain_west, gain_north, gain_south = map(
            trim, (gain_own, gain_east, gain_west, gain_north, gain_south)
        )
    out_height[...] = height

    for copy in seconds:
        copy.wait_recv()
    solve(work, second_in, out_tracer, heat)

    surface_all[0] = jnp.concatenate([out_tracer[0], height], axis=0).astype(BF16)

    def share(slot, _):
        copy_to(
            slot, surface_all.at[0], surface_all.at[slot], surface_sems.at[0], surface_sems.at[1]
        ).start()
        return 0

    lax.fori_loop(1, count, share, 0)

    high = 2 * rows
    spot = iota((sources, count * high), 1)
    spot_row = wrapped(me - idiv(spot, high), count) * rows + imod(spot, rows)
    spot_field = idiv(imod(spot, high), rows)
    picks = []
    for k in range(links):
        match = spot_row == target[k]
        for f in range(2):
            picks.append(jnp.where(match & (spot_field == f), 1.0, 0.0))
    out_picks[...] = jnp.concatenate(picks, axis=0).astype(BF16)

    everyone = copy_to(
        1,
        surface_all.at[pl.ds(1, count - 1)],
        surface_all.at[pl.ds(1, count - 1)],
        surface_sems.at[0],
        surface_sems.at[1],
    )
    everyone.wait_recv()
    for copy in edges + bases + forces + seconds:
        copy.wait_send()
    whole.wait_send()
    everyone.wait_send()


def finish(
    tracer_ref,
    height_ref,
    weight_ref,
    surface_ref,
    picks_ref,
    out_tracer,
    out_height,
    out_air,
    returned,
    sems,
):
    sources, links, cols, width = weight_ref.shape[1:]
    pair = 2 if sources % 2 == 0 else 1
    stores = [
        pltpu.make_async_copy(tracer_ref, out_tracer, sems.at[0]),
        pltpu.make_async_copy(height_ref, out_height, sems.at[1]),
    ]
    for copy in stores:
        copy.start()
    chosen = jnp.dot(
        picks_ref[...], surface_ref[...].reshape(-1, width), preferred_element_type=F32
    ).astype(BF16)
    both = 2 * sources
    chosen = jnp.concatenate([chosen[k * both : (k + 1) * both] for k in range(links)], axis=1)
    results = []
    for p in range(sources // pair):
        rhs = jnp.concatenate(
            [
                weight_ref[0, pl.ds(p * pair, pair), k].reshape(pair * cols, width)
                for k in range(links)
            ],
            axis=1,
        )
        full = lax.dot_general(
            chosen, rhs, (((1,), (1,)), ((), ())), preferred_element_type=F32
        ).reshape(2, sources, pair * cols)
        belongs = iota(full.shape, 1) == p * pair + idiv(iota(full.shape, 2), cols)
        results.append(jnp.sum(jnp.where(belongs, full, 0.0), axis=1))
    returned[0] = jnp.concatenate(results, axis=1).astype(BF16)
    last = pltpu.make_async_copy(returned, out_air, sems.at[2])
    last.start()
    for copy in stores + [last]:
        copy.wait()


def shards(count, blocks_dom, air, weights, targets, tracer, mix, height, flow, wet):
    fields = air.shape[1]
    sources, links = weights.shape[1:3]
    levels, rows, width = tracer.shape
    sides = 2 * -(-NSTEP * NSUB // rows)
    column = pltpu.VMEM((levels, rows, width), F32)
    spec = pl.BlockSpec(memory_space=pltpu.VMEM)
    dma = pltpu.SemaphoreType.DMA
    space = pl.BlockSpec(memory_space=pltpu.HBM)
    out_air = jax.ShapeDtypeStruct((1, 2, air.shape[2]), BF16)
    out_tracer = jax.ShapeDtypeStruct(tracer.shape, F32)
    out_height = jax.ShapeDtypeStruct(height.shape, F32)
    operands = (air, weights, jnp.swapaxes(targets, 1, 2), tracer, mix, height, flow, wet)
    operands = [pltpu.with_memory_space_constraint(v, pltpu.HBM) for v in operands]
    parts = pl.pallas_call(
        functools.partial(kernel, count, blocks_dom),
        out_shape=(
            out_tracer,
            out_height,
            jax.ShapeDtypeStruct(weights.shape, BF16),
            jax.ShapeDtypeStruct((count, 2 * rows, width), BF16),
            jax.ShapeDtypeStruct((2 * sources * links, count * 2 * rows), BF16),
        ),
        in_specs=[space] * 8,
        out_specs=(spec,) * 5,
        scratch_shapes=[
            pltpu.VMEM(air.shape, BF16),
            pltpu.VMEM((1, links, sources), jnp.int32),
            pltpu.VMEM(tracer.shape, F32),
            pltpu.VMEM(mix.shape, F32),
            pltpu.VMEM(wet.shape, jnp.int32),
            pltpu.VMEM((sources * links * fields, width), F32),
            pltpu.VMEM((count, fields * rows, width), BF16),
            pltpu.VMEM((count, fields * rows, width), BF16),
            pltpu.VMEM((4 * rows, width), F32),
            pltpu.VMEM((sides, 4 * rows, width), F32),
            pltpu.VMEM((2, levels + rows, width), F32),
            pltpu.VMEM((2, levels + rows, width), F32),
            pltpu.VMEM((3 * rows, width), F32),
            pltpu.VMEM((sides, 3 * rows, width), F32),
            pltpu.VMEM((2, levels, width), F32),
            pltpu.VMEM((2, levels, width), F32),
            column,
            column,
            column,
            column,
            column,
            dma((8,)),
            dma((sources,)),
            dma((2,)),
            dma((sides,)),
            dma((sides,)),
            dma((2,)),
            dma((2,)),
            dma((sides,)),
            dma((sides,)),
            dma((2,)),
            dma((2,)),
            dma((2,)),
        ],
        compiler_params=pltpu.CompilerParams(
            collective_id=0, has_side_effects=True, vmem_limit_bytes=32 * 1024 * 1024
        ),
    )(*operands)
    return pl.pallas_call(
        finish,
        out_shape=(out_tracer, out_height, out_air),
        in_specs=[spec] * 5,
        out_specs=(space,) * 3,
        scratch_shapes=[pltpu.VMEM(out_air.shape, BF16), dma((3,))],
        compiler_params=pltpu.CompilerParams(vmem_limit_bytes=32 * 1024 * 1024),
    )(*parts)


def solution(mesh):
    count = mesh.shape["comp"] * mesh.shape["dom"]
    return jax.shard_map(
        functools.partial(shards, count, mesh.shape["dom"]),
        mesh=mesh,
        in_specs=(
            P("comp", None, "dom"),
            P("comp", "dom", None, None, None),
            P("comp", "dom", None),
            P(None, ("comp", "dom"), None),
            P(None, ("comp", "dom"), None),
            P(("comp", "dom"), None),
            P(None, ("comp", "dom"), None),
            P(("comp", "dom"), None),
        ),
        out_specs=(
            P(None, ("comp", "dom"), None),
            P(("comp", "dom"), None),
            P("comp", None, "dom"),
        ),
        check_vma=False,
    )
```

```python
import functools

import jax
import jax.numpy as jnp
from jax import lax
from jax.experimental import pallas as pl
from jax.experimental.pallas import tpu as pltpu
from jax.sharding import PartitionSpec as P

NSTEP = 2
NSUB = 8

wave_gain = 0.35
stress_gain = 0.1
fresh_gain = 0.1
spread_gain = 0.2
heating_gain = 0.5

MESH = pl.DeviceIdType.MESH
F32 = jnp.float32
BF16 = jnp.bfloat16


def idiv(value, by):
    if by & (by - 1) == 0:
        return lax.shift_right_logical(value, jnp.full_like(value, by.bit_length() - 1))
    return value // by


def imod(value, by):
    if by & (by - 1) == 0:
        return value & (by - 1)
    return value % by


def wrapped(value, count):
    value = jnp.where(value >= count, value - count, value)
    return jnp.where(value < 0, value + count, value)


def iota(shape, dim):
    return lax.broadcasted_iota(jnp.int32, shape, dim)


def east(v):
    return pltpu.roll(v, v.shape[-1] - 1, v.ndim - 1)


def west(v):
    return pltpu.roll(v, 1, v.ndim - 1)


def north(v):
    return pltpu.roll(v, v.shape[-2] - 1, v.ndim - 2)


def south(v):
    return pltpu.roll(v, 1, v.ndim - 2)


def kernel(
    groups,
    blocks_dom,
    air_hbm,
    weight_hbm,
    target_hbm,
    tracer_hbm,
    mix_hbm,
    height_hbm,
    flow_hbm,
    wet_hbm,
    out_tracer,
    out_height,
    weight_ref,
    surface_all,
    out_picks,
    air_ref,
    target_ref,
    tracer_ref,
    mix_ref,
    wet_ref,
    terms,
    dense,
    flux_in,
    middle_out,
    middle_in,
    base_out,
    base_in,
    edge_out,
    edge_in,
    force_out,
    force_in,
    second_out,
    second_in,
    inverse,
    carry,
    ratio,
    response,
    work,
    load_sems,
    weight_sems,
    flux_sems,
    middle_sems,
    base_send,
    base_recv,
    edge_send,
    edge_recv,
    force_send,
    force_recv,
    second_send,
    second_recv,
    column_sems,
    surface_sems,
):
    group, block = lax.axis_index("comp"), lax.axis_index("dom")
    me = group * blocks_dom + block
    count = groups * blocks_dom
    fields = air_ref.shape[1]
    sources, links, cols, width = weight_ref.shape[1:]
    levels, rows = tracer_ref.shape[:2]
    steps = NSTEP * NSUB
    reach = -(-steps // rows)
    offsets = [d for d in range(-reach, reach + 1) if d != 0]
    pair = 2 if sources % 2 == 0 else 1

    def beside(offset):
        peer = lax.rem(me + offset + count, count)
        return (peer // blocks_dom, lax.rem(peer, blocks_dom))

    def in_group(offset):
        return (group, lax.rem(block + offset, blocks_dom))

    def across(offset):
        return (lax.rem(group + offset, groups), block)

    def copy_to(peer, src, dst, send, recv):
        return pltpu.make_async_remote_copy(
            src_ref=src,
            dst_ref=dst,
            send_sem=send,
            recv_sem=recv,
            device_id=peer,
            device_id_type=MESH,
        )

    pairs = sources // pair
    weight_loads = [
        pltpu.make_async_copy(
            weight_hbm.at[:, pl.ds(p * pair, pair)],
            weight_ref.at[:, pl.ds(p * pair, pair)],
            weight_sems.at[p],
        )
        for p in range(pairs)
    ]
    loads = [
        pltpu.make_async_copy(src, dst, load_sems.at[i])
        for i, (src, dst) in enumerate(
            [
                (air_hbm, air_ref),
                (target_hbm, target_ref),
                (wet_hbm, wet_ref),
                (tracer_hbm, tracer_ref),
                (height_hbm, base_out.at[pl.ds(0, rows)]),
                (flow_hbm.at[0], base_out.at[pl.ds(rows, rows)]),
                (flow_hbm.at[1], base_out.at[pl.ds(2 * rows, rows)]),
                (mix_hbm, mix_ref),
            ]
        )
    ]
    for copy in loads[:2] + weight_loads + loads[2:]:
        copy.start()

    barrier = pltpu.get_barrier_semaphore()

    def greet(peer):
        pl.semaphore_signal(barrier, inc=1, device_id=peer, device_id_type=MESH)

    def greet_group(offset, _):
        greet(in_group(offset))
        return 0

    lax.fori_loop(1, blocks_dom, greet_group, 0)
    for offset in range(1, groups):
        greet(across(offset))
    for offset in offsets:
        greet(beside(offset))

    loads[0].wait()
    loads[1].wait()
    exchange = air_ref[0].astype(F32)
    group_rows = pair * fields
    own = idiv(iota((group_rows, pair * cols), 0), fields) == idiv(
        iota((group_rows, pair * cols), 1), cols
    )
    for p in range(pairs):
        weight_loads[p].wait()
        part = exchange[:, p * pair * cols : (p + 1) * pair * cols]
        lhs = jnp.where(own, jnp.concatenate([part] * pair, axis=0), 0.0).astype(BF16)
        for k in range(links):
            rhs = weight_ref[0, pl.ds(p * pair, pair), k].reshape(pair * cols, width)
            terms[pl.ds((p * links + k) * group_rows, group_rows), :] = jnp.dot(
                lhs, rhs, preferred_element_type=F32
            )
    every = sources * links * fields
    diagonal = iota((sources, sources), 0) == iota((sources, sources), 1)
    numbers = target_ref[0].astype(F32)
    target = [
        jnp.sum(jnp.where(diagonal, numbers[k : k + 1], 0.0), axis=1, keepdims=True).astype(
            jnp.int32
        )
        for k in range(links)
    ]
    lane = iota((sources, every), 1)
    lane_field = imod(lane, fields)
    lane_source = idiv(lane, group_rows * links) * pair + imod(idiv(lane, fields), pair)
    lane_link = imod(idiv(lane, group_rows), links)
    here = lane_source == iota((sources, every), 0)
    lane_target = jnp.zeros((sources, every), jnp.int32)
    for k in range(links):
        lane_target = jnp.where(here & (lane_link == k), target[k], lane_target)
    lane_target = jnp.sum(lane_target, axis=0, keepdims=True)
    lane_key = lane_target * fields + lane_field[:1]
    value = terms[...]
    upper = value.astype(BF16)
    lower = (value - upper.astype(F32)).astype(BF16)
    split = jnp.concatenate([upper, lower], axis=0)

    for copy in loads[2:4]:
        copy.wait()
    wet = wet_ref[...].astype(F32)
    base_out[pl.ds(3 * rows, rows), :] = wet
    edge_out[0, pl.ds(0, levels), :] = tracer_ref[:, rows - 1, :]
    edge_out[1, pl.ds(0, levels), :] = tracer_ref[:, 0, :]
    edge_out[0, pl.ds(levels, rows), :] = wet
    edge_out[1, pl.ds(levels, rows), :] = wet

    pl.semaphore_wait(barrier, blocks_dom - 1 + groups - 1 + len(offsets))

    edges = [
        copy_to(beside(1), edge_out.at[0], edge_in.at[0], edge_send.at[0], edge_recv.at[0]),
        copy_to(beside(-1), edge_out.at[1], edge_in.at[1], edge_send.at[1], edge_recv.at[1]),
    ]
    for copy in edges:
        copy.start()

    chunk = 2 if blocks_dom % 2 == 0 else 1
    shape = (chunk, groups, fields, rows, every)

    def place(c, _):
        to_block = wrapped(iota(shape, 0) + (c * chunk + block), blocks_dom)
        to_group = wrapped(iota(shape, 1) + group, groups)
        row_key = ((to_group * blocks_dom + to_block) * rows + iota(shape, 3)) * fields
        row_key = (row_key + iota(shape, 2)).reshape(chunk * groups * fields * rows, every)
        hot = jnp.where(row_key == lane_key, 1.0, 0.0).astype(BF16)
        hot = jnp.concatenate([hot, hot], axis=1)
        placed = jnp.dot(hot, split, preferred_element_type=F32)
        dense[pl.ds(c * chunk, chunk)] = placed.astype(BF16).reshape(
            chunk, groups, fields * rows, width
        )
        for b in range(chunk):
            slot = c * chunk + b

            @pl.when(slot > 0)
            def _():
                copy_to(
                    in_group(slot),
                    dense.at[slot],
                    flux_in.at[slot],
                    flux_sems.at[0],
                    flux_sems.at[1],
                ).start()

        return 0

    lax.fori_loop(0, blocks_dom // chunk, place, 0)

    for copy in loads[4:]:
        copy.wait()
    bases = []
    for i, offset in enumerate(offsets):
        arrives = offsets.index(-offset)
        bases.append(
            copy_to(beside(offset), base_out, base_in.at[arrives], base_send.at[i], base_recv.at[arrives])
        )
    for copy in bases:
        copy.start()

    zero = jnp.zeros((rows, width), F32)
    last_ratio = None
    last_response = None
    for l in range(levels):
        up = mix_ref[l - 1] if l > 0 else zero
        down = mix_ref[l] if l < levels - 1 else zero
        pivot = 1.0 + up + down
        if l > 0:
            pivot = pivot - up * last_ratio
        inv = 1.0 / pivot
        inverse[l] = inv
        carry[l] = up * inv
        last_response = inv if l == 0 else up * inv * last_response
        response[l] = last_response
        last_ratio = down * inv
        ratio[l] = last_ratio
    for l in range(levels - 2, -1, -1):
        last_response = response[l] + ratio[l] * last_response
        response[l] = last_response

    for copy in edges:
        copy.wait_recv()
    row = iota((rows, width), 0)
    top = row == rows - 1
    bottom = row == 0
    wet_north = jnp.where(top, edge_in[1, pl.ds(levels, 1), :], north(wet))
    wet_south = jnp.where(bottom, edge_in[0, pl.ds(levels + rows - 1, 1), :], south(wet))
    inside_top = jnp.logical_not(top & (me == count - 1))
    inside_bottom = jnp.logical_not(bottom & (me == 0))
    mix_east = spread_gain * wet * east(wet)
    mix_west = spread_gain * wet * west(wet)
    mix_north = jnp.where(inside_top, spread_gain * wet * wet_north, 0.0)
    mix_south = jnp.where(inside_bottom, spread_gain * wet * wet_south, 0.0)
    mix_own = 1.0 - (mix_east + mix_west + mix_north + mix_south)

    def solve(source, halo, result, gain):
        swept = None
        for l in range(levels):
            v = source[l]
            v_north = jnp.where(top, halo[1, pl.ds(l, 1), :], north(v))
            v_south = jnp.where(bottom, halo[0, pl.ds(l, 1), :], south(v))
            explicit = (
                mix_own * v
                + mix_east * east(v)
                + mix_west * west(v)
                + mix_north * v_north
                + mix_south * v_south
            )
            if l == 0 and gain is not None:
                explicit = explicit + gain
            swept = explicit * inverse[l] if l == 0 else explicit * inverse[l] + carry[l] * swept
            result[l] = swept
        for l in range(levels - 2, -1, -1):
            swept = result[l] + ratio[l] * swept
            result[l] = swept

    solve(tracer_ref, edge_in, work, None)

    others = pl.ds(1, blocks_dom - 1)
    whole = copy_to(
        in_group(1), dense.at[others], flux_in.at[others], flux_sems.at[0], flux_sems.at[1]
    )
    whole.wait_recv()
    middles = []
    for j in list(range(1, groups)) + [0]:
        flux = dense[0, j].astype(F32)
        for o in range(1, blocks_dom):
            flux = flux + flux_in[o, j].astype(F32)
        if j > 0:
            middle_out[j] = flux.astype(BF16)
            middles.append(
                copy_to(
                    across(j),
                    middle_out.at[j],
                    middle_in.at[j],
                    middle_sems.at[0, j],
                    middle_sems.at[1, j],
                )
            )
            middles[-1].start()
    for j in range(1, groups):
        middles[j - 1].wait_recv()
        flux = flux + middle_in[j].astype(F32)
    heating = flux[0:rows]
    fresh = flux[rows : 2 * rows]
    force_out[pl.ds(0, rows), :] = fresh * wet
    force_out[pl.ds(rows, 2 * rows), :] = flux[2 * rows : 4 * rows]
    forces = []
    for i, offset in enumerate(offsets):
        arrives = offsets.index(-offset)
        forces.append(
            copy_to(
                beside(offset),
                force_out,
                force_in.at[arrives],
                force_send.at[i],
                force_recv.at[arrives],
            )
        )
    for copy in forces:
        copy.start()

    heat = heating_gain * heating * wet
    for l in range(levels):
        work[l] = work[l] + heat * response[l]
    second_out[0] = work[:, rows - 1, :]
    second_out[1] = work[:, 0, :]
    seconds = [
        copy_to(beside(1), second_out.at[0], second_in.at[0], second_send.at[0], second_recv.at[0]),
        copy_to(beside(-1), second_out.at[1], second_in.at[1], second_send.at[1], second_recv.at[1]),
    ]
    for copy in seconds:
        copy.start()

    for copy in bases:
        copy.wait_recv()

    def window(own_ref, arrived, start):
        parts = []
        for offset in range(-reach, reach + 1):
            if offset == 0:
                parts.append(own_ref[pl.ds(start, rows), :])
            else:
                parts.append(arrived[offsets.index(offset), pl.ds(start, rows), :])
        return jnp.concatenate(parts, axis=0)

    tall = (2 * reach + 1) * rows
    height = window(base_out, base_in, 0)
    flow_east = window(base_out, base_in, rows)
    flow_north = window(base_out, base_in, 2 * rows)
    wet_tall = window(base_out, base_in, 3 * rows)
    number = wrapped(me * rows - reach * rows + iota((tall, width), 0), count * rows)
    face_east = wet_tall * east(wet_tall)
    face_north = jnp.where(number == count * rows - 1, 0.0, wet_tall * north(wet_tall))
    face_west = west(face_east)
    face_south = south(face_north)
    square = wave_gain * wave_gain
    gain_east = square * face_east
    gain_west = square * face_west
    gain_north = square * face_north
    gain_south = square * face_south
    gain_own = gain_east + gain_west + gain_north + gain_south
    flow_east = wave_gain * face_east * flow_east
    flow_north = wave_gain * face_north * flow_north
    spread = flow_east - west(flow_east) + flow_north - south(flow_north)

    for copy in forces:
        copy.wait_recv()
    fresh_tall = fresh_gain * window(force_out, force_in, 0)
    push_east = (wave_gain * stress_gain) * face_east * window(force_out, force_in, rows)
    push_north = (wave_gain * stress_gain) * face_north * window(force_out, force_in, 2 * rows)
    push = push_east - west(push_east) + push_north - south(push_north)

    left = steps
    for stage in range(reach):
        turns = min(rows, left)
        left -= turns

        def subcycle(_, state):
            height, spread = state
            spread = (
                spread
                + push
                + gain_own * height
                - gain_east * east(height)
                - gain_west * west(height)
                - gain_north * north(height)
                - gain_south * south(height)
            )
            return height - spread + fresh_tall, spread

        height, spread = lax.fori_loop(0, turns, subcycle, (height, spread))
        trim = lambda v: v[rows:-rows]
        height, spread, push, fresh_tall = map(trim, (height, spread, push, fresh_tall))
        gain_own, gain_east, gain_west, gain_north, gain_south = map(
            trim, (gain_own, gain_east, gain_west, gain_north, gain_south)
        )
    out_height[...] = height

    for copy in seconds:
        copy.wait_recv()
    solve(work, second_in, out_tracer, heat)

    surface_all[0, 0] = jnp.concatenate([out_tracer[0], height], axis=0).astype(BF16)
    columns = [
        copy_to(
            across(j),
            surface_all.at[0, 0],
            surface_all.at[0, j],
            column_sems.at[0, j],
            column_sems.at[1, j],
        )
        for j in range(1, groups)
    ]
    for copy in columns:
        copy.start()

    for copy in columns:
        copy.wait_recv()

    def share(slot, _):
        copy_to(
            in_group(slot),
            surface_all.at[0],
            surface_all.at[slot],
            surface_sems.at[0],
            surface_sems.at[1],
        ).start()
        return 0

    lax.fori_loop(1, blocks_dom, share, 0)

    high = 2 * rows
    spot = iota((sources, count * high), 1)
    spot_block = wrapped(block - idiv(spot, high * groups), blocks_dom)
    spot_group = wrapped(group - imod(idiv(spot, high), groups), groups)
    spot_row = (spot_group * blocks_dom + spot_block) * rows + imod(spot, rows)
    spot_field = idiv(imod(spot, high), rows)
    picks = []
    for k in range(links):
        match = spot_row == target[k]
        for f in range(2):
            picks.append(jnp.where(match & (spot_field == f), 1.0, 0.0))
    out_picks[...] = jnp.concatenate(picks, axis=0).astype(BF16)

    everyone = copy_to(
        in_group(1),
        surface_all.at[others],
        surface_all.at[others],
        surface_sems.at[0],
        surface_sems.at[1],
    )
    for copy in edges + bases + forces + seconds + middles + columns:
        copy.wait_send()
    whole.wait_send()
    everyone.wait_recv()
    everyone.wait_send()


def finish(
    tracer_ref,
    height_ref,
    weight_ref,
    surface_ref,
    picks_ref,
    out_tracer,
    out_height,
    out_air,
    returned,
    sems,
):
    sources, links, cols, width = weight_ref.shape[1:]
    pair = 2 if sources % 2 == 0 else 1
    stores = [
        pltpu.make_async_copy(tracer_ref, out_tracer, sems.at[0]),
        pltpu.make_async_copy(height_ref, out_height, sems.at[1]),
    ]
    for copy in stores:
        copy.start()
    chosen = jnp.dot(
        picks_ref[...], surface_ref[...].reshape(-1, width), preferred_element_type=F32
    ).astype(BF16)
    both = 2 * sources
    chosen = jnp.concatenate([chosen[k * both : (k + 1) * both] for k in range(links)], axis=1)
    results = []
    for p in range(sources // pair):
        rhs = jnp.concatenate(
            [
                weight_ref[0, pl.ds(p * pair, pair), k].reshape(pair * cols, width)
                for k in range(links)
            ],
            axis=1,
        )
        full = lax.dot_general(
            chosen, rhs, (((1,), (1,)), ((), ())), preferred_element_type=F32
        ).reshape(2, sources, pair * cols)
        belongs = iota(full.shape, 1) == p * pair + idiv(iota(full.shape, 2), cols)
        results.append(jnp.sum(jnp.where(belongs, full, 0.0), axis=1))
    returned[0] = jnp.concatenate(results, axis=1).astype(BF16)
    last = pltpu.make_async_copy(returned, out_air, sems.at[2])
    last.start()
    for copy in stores + [last]:
        copy.wait()


def shards(groups, blocks_dom, air, weights, targets, tracer, mix, height, flow, wet):
    fields = air.shape[1]
    sources, links = weights.shape[1:3]
    levels, rows, width = tracer.shape
    sides = 2 * -(-NSTEP * NSUB // rows)
    column = pltpu.VMEM((levels, rows, width), F32)
    spec = pl.BlockSpec(memory_space=pltpu.VMEM)
    dma = pltpu.SemaphoreType.DMA
    space = pl.BlockSpec(memory_space=pltpu.HBM)
    out_air = jax.ShapeDtypeStruct((1, 2, air.shape[2]), BF16)
    out_tracer = jax.ShapeDtypeStruct(tracer.shape, F32)
    out_height = jax.ShapeDtypeStruct(height.shape, F32)
    operands = (air, weights, jnp.swapaxes(targets, 1, 2), tracer, mix, height, flow, wet)
    operands = [pltpu.with_memory_space_constraint(v, pltpu.HBM) for v in operands]
    parts = pl.pallas_call(
        functools.partial(kernel, groups, blocks_dom),
        out_shape=(
            out_tracer,
            out_height,
            jax.ShapeDtypeStruct(weights.shape, BF16),
            jax.ShapeDtypeStruct((blocks_dom, groups, 2 * rows, width), BF16),
            jax.ShapeDtypeStruct((2 * sources * links, groups * blocks_dom * 2 * rows), BF16),
        ),
        in_specs=[space] * 8,
        out_specs=(spec,) * 5,
        scratch_shapes=[
            pltpu.VMEM(air.shape, BF16),
            pltpu.VMEM((1, links, sources), jnp.int32),
            pltpu.VMEM(tracer.shape, F32),
            pltpu.VMEM(mix.shape, F32),
            pltpu.VMEM(wet.shape, jnp.int32),
            pltpu.VMEM((sources * links * fields, width), F32),
            pltpu.VMEM((blocks_dom, groups, fields * rows, width), BF16),
            pltpu.VMEM((blocks_dom, groups, fields * rows, width), BF16),
            pltpu.VMEM((groups, fields * rows, width), BF16),
            pltpu.VMEM((groups, fields * rows, width), BF16),
            pltpu.VMEM((4 * rows, width), F32),
            pltpu.VMEM((sides, 4 * rows, width), F32),
            pltpu.VMEM((2, levels + rows, width), F32),
            pltpu.VMEM((2, levels + rows, width), F32),
            pltpu.VMEM((3 * rows, width), F32),
            pltpu.VMEM((sides, 3 * rows, width), F32),
            pltpu.VMEM((2, levels, width), F32),
            pltpu.VMEM((2, levels, width), F32),
            column,
            column,
            column,
            column,
            column,
            dma((8,)),
            dma((sources,)),
            dma((2,)),
            dma((2, groups)),
            dma((sides,)),
            dma((sides,)),
            dma((2,)),
            dma((2,)),
            dma((sides,)),
            dma((sides,)),
            dma((2,)),
            dma((2,)),
            dma((2, groups)),
            dma((2,)),
        ],
        compiler_params=pltpu.CompilerParams(
            collective_id=0, has_side_effects=True, vmem_limit_bytes=32 * 1024 * 1024
        ),
    )(*operands)
    return pl.pallas_call(
        finish,
        out_shape=(out_tracer, out_height, out_air),
        in_specs=[spec] * 5,
        out_specs=(space,) * 3,
        scratch_shapes=[pltpu.VMEM(out_air.shape, BF16), dma((3,))],
        compiler_params=pltpu.CompilerParams(vmem_limit_bytes=32 * 1024 * 1024),
    )(*parts)


def solution(mesh):
    return jax.shard_map(
        functools.partial(shards, mesh.shape["comp"], mesh.shape["dom"]),
        mesh=mesh,
        in_specs=(
            P("comp", None, "dom"),
            P("comp", "dom", None, None, None),
            P("comp", "dom", None),
            P(None, ("comp", "dom"), None),
            P(None, ("comp", "dom"), None),
            P(("comp", "dom"), None),
            P(None, ("comp", "dom"), None),
            P(("comp", "dom"), None),
        ),
        out_specs=(
            P(None, ("comp", "dom"), None),
            P(("comp", "dom"), None),
            P("comp", None, "dom"),
        ),
        check_vma=False,
    )
```

```python
import functools

import jax
import jax.numpy as jnp
from jax import lax
from jax.experimental import pallas as pl
from jax.experimental.pallas import tpu as pltpu
from jax.sharding import PartitionSpec as P

NSTEP = 2
NSUB = 8

wave_gain = 0.35
stress_gain = 0.1
fresh_gain = 0.1
spread_gain = 0.2
heating_gain = 0.5

MESH = pl.DeviceIdType.MESH
F32 = jnp.float32
BF16 = jnp.bfloat16


def idiv(value, by):
    if by & (by - 1) == 0:
        return lax.shift_right_logical(value, jnp.full_like(value, by.bit_length() - 1))
    return value // by


def imod(value, by):
    if by & (by - 1) == 0:
        return value & (by - 1)
    return value % by


def wrapped(value, count):
    value = jnp.where(value >= count, value - count, value)
    return jnp.where(value < 0, value + count, value)


def iota(shape, dim):
    return lax.broadcasted_iota(jnp.int32, shape, dim)


def east(v):
    return pltpu.roll(v, v.shape[-1] - 1, v.ndim - 1)


def west(v):
    return pltpu.roll(v, 1, v.ndim - 1)


def north(v):
    return pltpu.roll(v, v.shape[-2] - 1, v.ndim - 2)


def south(v):
    return pltpu.roll(v, 1, v.ndim - 2)


def kernel(
    count,
    blocks_dom,
    air_hbm,
    weight_hbm,
    target_hbm,
    tracer_hbm,
    mix_hbm,
    height_hbm,
    flow_hbm,
    wet_hbm,
    out_tracer,
    out_height,
    weight_ref,
    surface_all,
    out_picks,
    air_ref,
    target_ref,
    tracer_ref,
    mix_ref,
    wet_ref,
    terms,
    dense,
    flux_in,
    base_out,
    base_in,
    edge_out,
    edge_in,
    force_out,
    force_in,
    second_out,
    second_in,
    inverse,
    carry,
    ratio,
    response,
    work,
    load_sems,
    weight_sems,
    flux_sems,
    base_send,
    base_recv,
    edge_send,
    edge_recv,
    force_send,
    force_recv,
    second_send,
    second_recv,
    surface_sems,
):
    group, block = lax.axis_index("comp"), lax.axis_index("dom")
    me = group * blocks_dom + block
    fields = air_ref.shape[1]
    sources, links, cols, width = weight_ref.shape[1:]
    levels, rows = tracer_ref.shape[:2]
    steps = NSTEP * NSUB
    reach = -(-steps // rows)
    offsets = [d for d in range(-reach, reach + 1) if d != 0]
    pair = 2 if sources % 2 == 0 else 1

    def device(offset):
        peer = lax.rem(me + offset + count, count)
        return (peer // blocks_dom, lax.rem(peer, blocks_dom))

    def copy_to(offset, src, dst, send, recv):
        return pltpu.make_async_remote_copy(
            src_ref=src,
            dst_ref=dst,
            send_sem=send,
            recv_sem=recv,
            device_id=device(offset),
            device_id_type=MESH,
        )

    pairs = sources // pair
    weight_loads = [
        pltpu.make_async_copy(
            weight_hbm.at[:, pl.ds(p * pair, pair)],
            weight_ref.at[:, pl.ds(p * pair, pair)],
            weight_sems.at[p],
        )
        for p in range(pairs)
    ]
    loads = [
        pltpu.make_async_copy(src, dst, load_sems.at[i])
        for i, (src, dst) in enumerate(
            [
                (air_hbm, air_ref),
                (target_hbm, target_ref),
                (wet_hbm, wet_ref),
                (tracer_hbm, tracer_ref),
                (height_hbm, base_out.at[pl.ds(0, rows)]),
                (flow_hbm.at[0], base_out.at[pl.ds(rows, rows)]),
                (flow_hbm.at[1], base_out.at[pl.ds(2 * rows, rows)]),
                (mix_hbm, mix_ref),
            ]
        )
    ]
    for copy in loads[:2] + weight_loads + loads[2:]:
        copy.start()

    barrier = pltpu.get_barrier_semaphore()

    def greet(offset, _):
        pl.semaphore_signal(barrier, inc=1, device_id=device(offset), device_id_type=MESH)
        return 0

    lax.fori_loop(1, count, greet, 0)

    loads[0].wait()
    loads[1].wait()
    exchange = air_ref[0].astype(F32)
    group_rows = pair * fields
    own = idiv(iota((group_rows, pair * cols), 0), fields) == idiv(
        iota((group_rows, pair * cols), 1), cols
    )
    for p in range(pairs):
        weight_loads[p].wait()
        part = exchange[:, p * pair * cols : (p + 1) * pair * cols]
        lhs = jnp.where(own, jnp.concatenate([part] * pair, axis=0), 0.0).astype(BF16)
        for k in range(links):
            rhs = weight_ref[0, pl.ds(p * pair, pair), k].reshape(pair * cols, width)
            terms[pl.ds((p * links + k) * group_rows, group_rows), :] = jnp.dot(
                lhs, rhs, preferred_element_type=F32
            )
    every = sources * links * fields
    diagonal = iota((sources, sources), 0) == iota((sources, sources), 1)
    numbers = target_ref[0].astype(F32)
    target = [
        jnp.sum(jnp.where(diagonal, numbers[k : k + 1], 0.0), axis=1, keepdims=True).astype(
            jnp.int32
        )
        for k in range(links)
    ]
    lane = iota((sources, every), 1)
    lane_field = imod(lane, fields)
    lane_source = idiv(lane, group_rows * links) * pair + imod(idiv(lane, fields), pair)
    lane_link = imod(idiv(lane, group_rows), links)
    here = lane_source == iota((sources, every), 0)
    lane_target = jnp.zeros((sources, every), jnp.int32)
    for k in range(links):
        lane_target = jnp.where(here & (lane_link == k), target[k], lane_target)
    lane_target = jnp.sum(lane_target, axis=0, keepdims=True)
    lane_key = lane_target * fields + lane_field[:1]
    value = terms[...]
    upper = value.astype(BF16)
    lower = (value - upper.astype(F32)).astype(BF16)
    split = jnp.concatenate([upper, lower], axis=0)

    for copy in loads[2:4]:
        copy.wait()
    wet = wet_ref[...].astype(F32)
    base_out[pl.ds(3 * rows, rows), :] = wet
    edge_out[0, pl.ds(0, levels), :] = tracer_ref[:, rows - 1, :]
    edge_out[1, pl.ds(0, levels), :] = tracer_ref[:, 0, :]
    edge_out[0, pl.ds(levels, rows), :] = wet
    edge_out[1, pl.ds(levels, rows), :] = wet

    pl.semaphore_wait(barrier, count - 1)

    edges = [
        copy_to(1, edge_out.at[0], edge_in.at[0], edge_send.at[0], edge_recv.at[0]),
        copy_to(-1, edge_out.at[1], edge_in.at[1], edge_send.at[1], edge_recv.at[1]),
    ]
    for copy in edges:
        copy.start()

    chunk = 8 if count % 8 == 0 else 1
    shape = (chunk, fields, rows, every)

    chunks = count // chunk

    def place(turn, _):
        c = lax.rem(turn + 1, chunks)
        slot = iota(shape, 0) + c * chunk
        row_key = (wrapped(slot + me, count) * rows + iota(shape, 2)) * fields + iota(shape, 1)
        row_key = row_key.reshape(chunk * fields * rows, every)
        hot = jnp.where(row_key == lane_key, 1.0, 0.0).astype(BF16)
        hot = jnp.concatenate([hot, hot], axis=1)
        placed = jnp.dot(hot, split, preferred_element_type=F32)
        dense[pl.ds(c * chunk, chunk)] = placed.astype(BF16).reshape(
            chunk, fields * rows, width
        )

        def send(b, _):
            slot = c * chunk + b

            @pl.when(slot > 0)
            def _():
                copy_to(
                    slot, dense.at[slot], flux_in.at[slot], flux_sems.at[0], flux_sems.at[1]
                ).start()

            return 0

        lax.fori_loop(0, chunk, send, 0)
        return 0

    lax.fori_loop(0, chunks, place, 0)

    for copy in loads[4:]:
        copy.wait()
    bases = []
    for i, offset in enumerate(offsets):
        arrives = offsets.index(-offset)
        bases.append(
            copy_to(offset, base_out, base_in.at[arrives], base_send.at[i], base_recv.at[arrives])
        )
    for copy in bases:
        copy.start()

    zero = jnp.zeros((rows, width), F32)
    last_ratio = None
    last_response = None
    for l in range(levels):
        up = mix_ref[l - 1] if l > 0 else zero
        down = mix_ref[l] if l < levels - 1 else zero
        pivot = 1.0 + up + down
        if l > 0:
            pivot = pivot - up * last_ratio
        inv = 1.0 / pivot
        inverse[l] = inv
        carry[l] = up * inv
        last_response = inv if l == 0 else up * inv * last_response
        response[l] = last_response
        last_ratio = down * inv
        ratio[l] = last_ratio
    for l in range(levels - 2, -1, -1):
        last_response = response[l] + ratio[l] * last_response
        response[l] = last_response

    for copy in edges:
        copy.wait_recv()
    row = iota((rows, width), 0)
    top = row == rows - 1
    bottom = row == 0
    wet_north = jnp.where(top, edge_in[1, pl.ds(levels, 1), :], north(wet))
    wet_south = jnp.where(bottom, edge_in[0, pl.ds(levels + rows - 1, 1), :], south(wet))
    inside_top = jnp.logical_not(top & (me == count - 1))
    inside_bottom = jnp.logical_not(bottom & (me == 0))
    mix_east = spread_gain * wet * east(wet)
    mix_west = spread_gain * wet * west(wet)
    mix_north = jnp.where(inside_top, spread_gain * wet * wet_north, 0.0)
    mix_south = jnp.where(inside_bottom, spread_gain * wet * wet_south, 0.0)
    mix_own = 1.0 - (mix_east + mix_west + mix_north + mix_south)

    def mixed(source, halo, l):
        v = source[l]
        v_north = jnp.where(top, halo[1, pl.ds(l, 1), :], north(v))
        v_south = jnp.where(bottom, halo[0, pl.ds(l, 1), :], south(v))
        return (
            (mix_own * v + mix_east * east(v))
            + mix_west * west(v)
            + (mix_north * v_north + mix_south * v_south)
        )

    def solve(explicit, result):
        swept = None
        for l in range(levels):
            swept = explicit(l) * inverse[l] if l == 0 else explicit(l) * inverse[l] + carry[l] * swept
            result[l] = swept
        for l in range(levels - 2, -1, -1):
            swept = result[l] + ratio[l] * swept
            result[l] = swept

    solve(lambda l: mixed(tracer_ref, edge_in, l), work)

    for copy in bases:
        copy.wait_recv()

    def window(own_ref, arrived, start):
        parts = []
        for offset in range(-reach, reach + 1):
            if offset == 0:
                parts.append(own_ref[pl.ds(start, rows), :])
            else:
                parts.append(arrived[offsets.index(offset), pl.ds(start, rows), :])
        return jnp.concatenate(parts, axis=0)

    tall = (2 * reach + 1) * rows
    height = window(base_out, base_in, 0)
    flow_east = window(base_out, base_in, rows)
    flow_north = window(base_out, base_in, 2 * rows)
    wet_tall = window(base_out, base_in, 3 * rows)
    number = wrapped(me * rows - reach * rows + iota((tall, width), 0), count * rows)
    face_east = wet_tall * east(wet_tall)
    face_north = jnp.where(number == count * rows - 1, 0.0, wet_tall * north(wet_tall))
    face_west = west(face_east)
    face_south = south(face_north)
    square = wave_gain * wave_gain
    gain_east = square * face_east
    gain_west = square * face_west
    gain_north = square * face_north
    gain_south = square * face_south
    gain_own = gain_east + gain_west + gain_north + gain_south
    flow_east = wave_gain * face_east * flow_east
    flow_north = wave_gain * face_north * flow_north
    spread = flow_east - west(flow_east) + flow_north - south(flow_north)

    whole = copy_to(
        1,
        dense.at[pl.ds(1, count - 1)],
        flux_in.at[pl.ds(1, count - 1)],
        flux_sems.at[0],
        flux_sems.at[1],
    )
    whole.wait_recv()

    flux_in[0] = dense[0]
    wide = 8 if count % 8 == 0 else 1

    def gather(turn, total):
        part = flux_in[pl.ds(turn * wide, wide)].astype(F32)
        return total + jnp.sum(part, axis=0)

    flux = lax.fori_loop(
        0, count // wide, gather, jnp.zeros((fields * rows, width), F32), unroll=count <= 32
    )
    heating = flux[0:rows]
    fresh = flux[rows : 2 * rows]
    force_out[pl.ds(0, rows), :] = fresh * wet
    force_out[pl.ds(rows, 2 * rows), :] = flux[2 * rows : 4 * rows]
    forces = []
    for i, offset in enumerate(offsets):
        arrives = offsets.index(-offset)
        forces.append(
            copy_to(
                offset, force_out, force_in.at[arrives], force_send.at[i], force_recv.at[arrives]
            )
        )
    for copy in forces:
        copy.start()

    heat = heating_gain * heating * wet
    for l in range(levels):
        work[l] = work[l] + heat * response[l]
    second_out[0] = work[:, rows - 1, :]
    second_out[1] = work[:, 0, :]
    seconds = [
        copy_to(1, second_out.at[0], second_in.at[0], second_send.at[0], second_recv.at[0]),
        copy_to(-1, second_out.at[1], second_in.at[1], second_send.at[1], second_recv.at[1]),
    ]
    for copy in seconds:
        copy.start()

    for copy in forces:
        copy.wait_recv()
    fresh_tall = fresh_gain * window(force_out, force_in, 0)
    push_east = (wave_gain * stress_gain) * face_east * window(force_out, force_in, rows)
    push_north = (wave_gain * stress_gain) * face_north * window(force_out, force_in, 2 * rows)
    push = push_east - west(push_east) + push_north - south(push_north)

    left = steps
    for stage in range(reach):
        turns = min(rows, left)
        left -= turns

        def subcycle(_, state):
            height, spread = state
            here = (spread + push) + gain_own * height
            sides = gain_east * east(height) + gain_west * west(height)
            ends = gain_north * north(height) + gain_south * south(height)
            spread = here - sides - ends
            return (height + fresh_tall) - spread, spread

        height, spread = lax.fori_loop(0, turns, subcycle, (height, spread), unroll=True)
        trim = lambda v: v[rows:-rows]
        height, spread, push, fresh_tall = map(trim, (height, spread, push, fresh_tall))
        gain_own, gain_east, gain_west, gain_north, gain_south = map(
            trim, (gain_own, gain_east, gain_west, gain_north, gain_south)
        )
    for copy in seconds:
        copy.wait_recv()
    surface = [jnp.zeros((rows, width), F32)] * 4
    for l in range(levels):
        explicit = mixed(work, second_in, l)
        if l == 0:
            explicit = explicit + heat
        out_tracer[l] = explicit
        surface[l % 4] = surface[l % 4] + response[l] * explicit
    surface = (surface[0] + surface[1]) + (surface[2] + surface[3])

    surface_all[0] = jnp.concatenate([surface, height], axis=0).astype(BF16)

    def share(slot, _):
        copy_to(
            slot, surface_all.at[0], surface_all.at[slot], surface_sems.at[0], surface_sems.at[1]
        ).start()
        return 0

    lax.fori_loop(1, count, share, 0)
    out_height[...] = height
    solve(lambda l: out_tracer[l], out_tracer)

    high = 2 * rows
    spot = iota((sources, count * high), 1)
    spot_row = wrapped(me - idiv(spot, high), count) * rows + imod(spot, rows)
    spot_field = idiv(imod(spot, high), rows)
    picks = []
    for k in range(links):
        match = spot_row == target[k]
        for f in range(2):
            picks.append(jnp.where(match & (spot_field == f), 1.0, 0.0))
    out_picks[...] = jnp.concatenate(picks, axis=0).astype(BF16)

    everyone = copy_to(
        1,
        surface_all.at[pl.ds(1, count - 1)],
        surface_all.at[pl.ds(1, count - 1)],
        surface_sems.at[0],
        surface_sems.at[1],
    )
    everyone.wait_recv()
    for copy in edges + bases + forces + seconds:
        copy.wait_send()
    whole.wait_send()
    everyone.wait_send()


def finish(
    tracer_ref,
    height_ref,
    weight_ref,
    surface_ref,
    picks_ref,
    out_tracer,
    out_height,
    out_air,
    returned,
    sems,
):
    sources, links, cols, width = weight_ref.shape[1:]
    pair = 2 if sources % 2 == 0 else 1
    stores = [
        pltpu.make_async_copy(tracer_ref, out_tracer, sems.at[0]),
        pltpu.make_async_copy(height_ref, out_height, sems.at[1]),
    ]
    for copy in stores:
        copy.start()
    chosen = jnp.dot(
        picks_ref[...], surface_ref[...].reshape(-1, width), preferred_element_type=F32
    ).astype(BF16)
    both = 2 * sources
    chosen = jnp.concatenate([chosen[k * both : (k + 1) * both] for k in range(links)], axis=1)
    results = []
    for p in range(sources // pair):
        rhs = jnp.concatenate(
            [
                weight_ref[0, pl.ds(p * pair, pair), k].reshape(pair * cols, width)
                for k in range(links)
            ],
            axis=1,
        )
        full = lax.dot_general(
            chosen, rhs, (((1,), (1,)), ((), ())), preferred_element_type=F32
        ).reshape(2, sources, pair * cols)
        belongs = iota(full.shape, 1) == p * pair + idiv(iota(full.shape, 2), cols)
        results.append(jnp.sum(jnp.where(belongs, full, 0.0), axis=1))
    returned[0] = jnp.concatenate(results, axis=1).astype(BF16)
    last = pltpu.make_async_copy(returned, out_air, sems.at[2])
    last.start()
    for copy in stores + [last]:
        copy.wait()


def shards(count, blocks_dom, air, weights, targets, tracer, mix, height, flow, wet):
    fields = air.shape[1]
    sources, links = weights.shape[1:3]
    levels, rows, width = tracer.shape
    sides = 2 * -(-NSTEP * NSUB // rows)
    column = pltpu.VMEM((levels, rows, width), F32)
    spec = pl.BlockSpec(memory_space=pltpu.VMEM)
    dma = pltpu.SemaphoreType.DMA
    space = pl.BlockSpec(memory_space=pltpu.HBM)
    out_air = jax.ShapeDtypeStruct((1, 2, air.shape[2]), BF16)
    out_tracer = jax.ShapeDtypeStruct(tracer.shape, F32)
    out_height = jax.ShapeDtypeStruct(height.shape, F32)
    operands = (air, weights, jnp.swapaxes(targets, 1, 2), tracer, mix, height, flow, wet)
    operands = [pltpu.with_memory_space_constraint(v, pltpu.HBM) for v in operands]
    parts = pl.pallas_call(
        functools.partial(kernel, count, blocks_dom),
        out_shape=(
            out_tracer,
            out_height,
            jax.ShapeDtypeStruct(weights.shape, BF16),
            jax.ShapeDtypeStruct((count, 2 * rows, width), BF16),
            jax.ShapeDtypeStruct((2 * sources * links, count * 2 * rows), BF16),
        ),
        in_specs=[space] * 8,
        out_specs=(spec,) * 5,
        scratch_shapes=[
            pltpu.VMEM(air.shape, BF16),
            pltpu.VMEM((1, links, sources), jnp.int32),
            pltpu.VMEM(tracer.shape, F32),
            pltpu.VMEM(mix.shape, F32),
            pltpu.VMEM(wet.shape, jnp.int32),
            pltpu.VMEM((sources * links * fields, width), F32),
            pltpu.VMEM((count, fields * rows, width), BF16),
            pltpu.VMEM((count, fields * rows, width), BF16),
            pltpu.VMEM((4 * rows, width), F32),
            pltpu.VMEM((sides, 4 * rows, width), F32),
            pltpu.VMEM((2, levels + rows, width), F32),
            pltpu.VMEM((2, levels + rows, width), F32),
            pltpu.VMEM((3 * rows, width), F32),
            pltpu.VMEM((sides, 3 * rows, width), F32),
            pltpu.VMEM((2, levels, width), F32),
            pltpu.VMEM((2, levels, width), F32),
            column,
            column,
            column,
            column,
            column,
            dma((8,)),
            dma((sources,)),
            dma((2,)),
            dma((sides,)),
            dma((sides,)),
            dma((2,)),
            dma((2,)),
            dma((sides,)),
            dma((sides,)),
            dma((2,)),
            dma((2,)),
            dma((2,)),
        ],
        compiler_params=pltpu.CompilerParams(
            collective_id=0, has_side_effects=True, vmem_limit_bytes=32 * 1024 * 1024
        ),
    )(*operands)
    return pl.pallas_call(
        finish,
        out_shape=(out_tracer, out_height, out_air),
        in_specs=[spec] * 5,
        out_specs=(space,) * 3,
        scratch_shapes=[pltpu.VMEM(out_air.shape, BF16), dma((3,))],
        compiler_params=pltpu.CompilerParams(vmem_limit_bytes=32 * 1024 * 1024),
    )(*parts)


def solution(mesh):
    count = mesh.shape["comp"] * mesh.shape["dom"]
    return jax.shard_map(
        functools.partial(shards, count, mesh.shape["dom"]),
        mesh=mesh,
        in_specs=(
            P("comp", None, "dom"),
            P("comp", "dom", None, None, None),
            P("comp", "dom", None),
            P(None, ("comp", "dom"), None),
            P(None, ("comp", "dom"), None),
            P(("comp", "dom"), None),
            P(None, ("comp", "dom"), None),
            P(("comp", "dom"), None),
        ),
        out_specs=(
            P(None, ("comp", "dom"), None),
            P(("comp", "dom"), None),
            P("comp", None, "dom"),
        ),
        check_vma=False,
    )
```

```python
import functools

import jax
import jax.numpy as jnp
from jax import lax
from jax.experimental import pallas as pl
from jax.experimental.pallas import tpu as pltpu
from jax.sharding import PartitionSpec as P

NSTEP = 2
NSUB = 8

wave_gain = 0.35
stress_gain = 0.1
fresh_gain = 0.1
spread_gain = 0.2
heating_gain = 0.5

MESH = pl.DeviceIdType.MESH
F32 = jnp.float32
BF16 = jnp.bfloat16


def idiv(value, by):
    if by & (by - 1) == 0:
        return lax.shift_right_logical(value, jnp.full_like(value, by.bit_length() - 1))
    return value // by


def imod(value, by):
    if by & (by - 1) == 0:
        return value & (by - 1)
    return value % by


def wrapped(value, count):
    value = jnp.where(value >= count, value - count, value)
    return jnp.where(value < 0, value + count, value)


def iota(shape, dim):
    return lax.broadcasted_iota(jnp.int32, shape, dim)


def east(v):
    return pltpu.roll(v, v.shape[-1] - 1, v.ndim - 1)


def west(v):
    return pltpu.roll(v, 1, v.ndim - 1)


def north(v):
    return pltpu.roll(v, v.shape[-2] - 1, v.ndim - 2)


def south(v):
    return pltpu.roll(v, 1, v.ndim - 2)


def kernel(
    count,
    blocks_dom,
    air_hbm,
    weight_hbm,
    target_hbm,
    tracer_hbm,
    mix_hbm,
    height_hbm,
    flow_hbm,
    wet_hbm,
    out_tracer,
    out_height,
    weight_ref,
    surface_all,
    out_picks,
    air_ref,
    target_ref,
    tracer_ref,
    mix_ref,
    wet_ref,
    terms,
    swap_out,
    swap_in,
    dense,
    flux_in,
    base_out,
    base_in,
    edge_out,
    edge_in,
    force_out,
    force_in,
    second_out,
    second_in,
    inverse,
    carry,
    ratio,
    response,
    work,
    load_sems,
    weight_sems,
    swap_sems,
    flux_sems,
    base_send,
    base_recv,
    edge_send,
    edge_recv,
    force_send,
    force_recv,
    second_send,
    second_recv,
    surface_sems,
):
    group, block = lax.axis_index("comp"), lax.axis_index("dom")
    me = group * blocks_dom + block
    fields = air_ref.shape[1]
    sources, links, cols, width = weight_ref.shape[1:]
    levels, rows = tracer_ref.shape[:2]
    steps = NSTEP * NSUB
    reach = -(-steps // rows)
    offsets = [d for d in range(-reach, reach + 1) if d != 0]
    pair = 2 if sources % 2 == 0 else 1

    def device(offset):
        peer = lax.rem(me + offset + count, count)
        return (peer // blocks_dom, lax.rem(peer, blocks_dom))

    def copy_to(offset, src, dst, send, recv):
        return pltpu.make_async_remote_copy(
            src_ref=src,
            dst_ref=dst,
            send_sem=send,
            recv_sem=recv,
            device_id=device(offset),
            device_id_type=MESH,
        )

    pairs = sources // pair
    weight_loads = [
        pltpu.make_async_copy(
            weight_hbm.at[:, pl.ds(p * pair, pair)],
            weight_ref.at[:, pl.ds(p * pair, pair)],
            weight_sems.at[p],
        )
        for p in range(pairs)
    ]
    loads = [
        pltpu.make_async_copy(src, dst, load_sems.at[i])
        for i, (src, dst) in enumerate(
            [
                (air_hbm, air_ref),
                (target_hbm, target_ref),
                (wet_hbm, wet_ref),
                (tracer_hbm, tracer_ref),
                (height_hbm, base_out.at[pl.ds(0, rows)]),
                (flow_hbm.at[0], base_out.at[pl.ds(rows, rows)]),
                (flow_hbm.at[1], base_out.at[pl.ds(2 * rows, rows)]),
                (mix_hbm, mix_ref),
            ]
        )
    ]
    for copy in loads[:2] + weight_loads + loads[2:]:
        copy.start()

    barrier = pltpu.get_barrier_semaphore()

    def greet(offset, _):
        pl.semaphore_signal(barrier, inc=1, device_id=device(offset), device_id_type=MESH)
        return 0

    lax.fori_loop(1, count, greet, 0)

    loads[0].wait()
    loads[1].wait()
    exchange = air_ref[0].astype(F32)
    group_rows = pair * fields
    own = idiv(iota((group_rows, pair * cols), 0), fields) == idiv(
        iota((group_rows, pair * cols), 1), cols
    )
    for p in range(pairs):
        weight_loads[p].wait()
        part = exchange[:, p * pair * cols : (p + 1) * pair * cols]
        lhs = jnp.where(own, jnp.concatenate([part] * pair, axis=0), 0.0).astype(BF16)
        for k in range(links):
            rhs = weight_ref[0, pl.ds(p * pair, pair), k].reshape(pair * cols, width)
            terms[pl.ds((p * links + k) * group_rows, group_rows), :] = jnp.dot(
                lhs, rhs, preferred_element_type=F32
            )
    every = sources * links * fields
    diagonal = iota((sources, sources), 0) == iota((sources, sources), 1)
    numbers = target_ref[0].astype(F32)
    target = [
        jnp.sum(jnp.where(diagonal, numbers[k : k + 1], 0.0), axis=1, keepdims=True).astype(
            jnp.int32
        )
        for k in range(links)
    ]
    lane = iota((sources, every), 1)
    lane_field = imod(lane, fields)
    lane_source = idiv(lane, group_rows * links) * pair + imod(idiv(lane, fields), pair)
    lane_link = imod(idiv(lane, group_rows), links)
    here = lane_source == iota((sources, every), 0)
    lane_target = jnp.zeros((sources, every), jnp.int32)
    for k in range(links):
        lane_target = jnp.where(here & (lane_link == k), target[k], lane_target)
    lane_target = jnp.sum(lane_target, axis=0, keepdims=True)
    lane_key = lane_target * fields + lane_field[:1]
    value = terms[...]
    upper = value.astype(BF16)
    lower = (value - upper.astype(F32)).astype(BF16)
    split = jnp.concatenate([upper, lower], axis=0)

    for copy in loads[2:4]:
        copy.wait()
    wet = wet_ref[...].astype(F32)
    base_out[pl.ds(3 * rows, rows), :] = wet
    edge_out[0, pl.ds(0, levels), :] = tracer_ref[:, rows - 1, :]
    edge_out[1, pl.ds(0, levels), :] = tracer_ref[:, 0, :]
    edge_out[0, pl.ds(levels, rows), :] = wet
    edge_out[1, pl.ds(levels, rows), :] = wet

    pl.semaphore_wait(barrier, count - 1)

    edges = [
        copy_to(1, edge_out.at[0], edge_in.at[0], edge_send.at[0], edge_recv.at[0]),
        copy_to(-1, edge_out.at[1], edge_in.at[1], edge_send.at[1], edge_recv.at[1]),
    ]
    for copy in edges:
        copy.start()

    chips = count // 2
    chip, core = me // 2, lax.rem(me, 2)
    sibling = 1 - 2 * core
    chunk = 8 if chips % 8 == 0 else 1
    chunks = chips // chunk
    shape = (chunk, fields, rows, every)

    def placed(c, place):
        to_chip = wrapped(iota(shape, 0) + (c * chunk + chip), chips)
        row_key = ((to_chip * 2 + place) * rows + iota(shape, 2)) * fields + iota(shape, 1)
        row_key = row_key.reshape(chunk * fields * rows, every)
        hot = jnp.where(row_key == lane_key, 1.0, 0.0).astype(BF16)
        hot = jnp.concatenate([hot, hot], axis=1)
        result = jnp.dot(hot, split, preferred_element_type=F32)
        return result.reshape(chunk, fields * rows, width)

    def swap(c):
        part = pl.ds(c * chunk, chunk)
        return copy_to(
            sibling, swap_out.at[part], swap_in.at[part], swap_sems.at[0, c], swap_sems.at[1, c]
        )

    def give(turn, _):
        c = lax.rem(turn + 1, chunks)
        swap_out[pl.ds(c * chunk, chunk)] = placed(c, 1 - core).astype(BF16)
        swap(c).start()
        return 0

    lax.fori_loop(0, chunks, give, 0)

    def keep(turn, _):
        c = lax.rem(turn + 1, chunks)
        part = pl.ds(c * chunk, chunk)
        mine = placed(c, core)
        swap(c).wait_recv()
        dense[part] = (mine + swap_in[part].astype(F32)).astype(BF16)

        def send(b, _):
            slot = c * chunk + b

            @pl.when(slot > 0)
            def _():
                copy_to(
                    2 * slot,
                    dense.at[slot],
                    flux_in.at[slot],
                    flux_sems.at[0],
                    flux_sems.at[1],
                ).start()

            return 0

        lax.fori_loop(0, chunk, send, 0)
        return 0

    lax.fori_loop(0, chunks, keep, 0)

    for copy in loads[4:]:
        copy.wait()
    bases = []
    for i, offset in enumerate(offsets):
        arrives = offsets.index(-offset)
        bases.append(
            copy_to(offset, base_out, base_in.at[arrives], base_send.at[i], base_recv.at[arrives])
        )
    for copy in bases:
        copy.start()

    zero = jnp.zeros((rows, width), F32)
    last_ratio = None
    last_response = None
    for l in range(levels):
        up = mix_ref[l - 1] if l > 0 else zero
        down = mix_ref[l] if l < levels - 1 else zero
        pivot = 1.0 + up + down
        if l > 0:
            pivot = pivot - up * last_ratio
        inv = 1.0 / pivot
        inverse[l] = inv
        carry[l] = up * inv
        last_response = inv if l == 0 else up * inv * last_response
        response[l] = last_response
        last_ratio = down * inv
        ratio[l] = last_ratio
    for l in range(levels - 2, -1, -1):
        last_response = response[l] + ratio[l] * last_response
        response[l] = last_response

    for copy in edges:
        copy.wait_recv()
    row = iota((rows, width), 0)
    top = row == rows - 1
    bottom = row == 0
    wet_north = jnp.where(top, edge_in[1, pl.ds(levels, 1), :], north(wet))
    wet_south = jnp.where(bottom, edge_in[0, pl.ds(levels + rows - 1, 1), :], south(wet))
    inside_top = jnp.logical_not(top & (me == count - 1))
    inside_bottom = jnp.logical_not(bottom & (me == 0))
    mix_east = spread_gain * wet * east(wet)
    mix_west = spread_gain * wet * west(wet)
    mix_north = jnp.where(inside_top, spread_gain * wet * wet_north, 0.0)
    mix_south = jnp.where(inside_bottom, spread_gain * wet * wet_south, 0.0)
    mix_own = 1.0 - (mix_east + mix_west + mix_north + mix_south)

    def mixed(source, halo, l):
        v = source[l]
        v_north = jnp.where(top, halo[1, pl.ds(l, 1), :], north(v))
        v_south = jnp.where(bottom, halo[0, pl.ds(l, 1), :], south(v))
        return (
            (mix_own * v + mix_east * east(v))
            + mix_west * west(v)
            + (mix_north * v_north + mix_south * v_south)
        )

    def solve(explicit, result):
        swept = None
        for l in range(levels):
            swept = explicit(l) * inverse[l] if l == 0 else explicit(l) * inverse[l] + carry[l] * swept
            result[l] = swept
        for l in range(levels - 2, -1, -1):
            swept = result[l] + ratio[l] * swept
            result[l] = swept

    solve(lambda l: mixed(tracer_ref, edge_in, l), work)

    for copy in bases:
        copy.wait_recv()

    def window(own_ref, arrived, start):
        parts = []
        for offset in range(-reach, reach + 1):
            if offset == 0:
                parts.append(own_ref[pl.ds(start, rows), :])
            else:
                parts.append(arrived[offsets.index(offset), pl.ds(start, rows), :])
        return jnp.concatenate(parts, axis=0)

    tall = (2 * reach + 1) * rows
    height = window(base_out, base_in, 0)
    flow_east = window(base_out, base_in, rows)
    flow_north = window(base_out, base_in, 2 * rows)
    wet_tall = window(base_out, base_in, 3 * rows)
    number = wrapped(me * rows - reach * rows + iota((tall, width), 0), count * rows)
    face_east = wet_tall * east(wet_tall)
    face_north = jnp.where(number == count * rows - 1, 0.0, wet_tall * north(wet_tall))
    face_west = west(face_east)
    face_south = south(face_north)
    square = wave_gain * wave_gain
    gain_east = square * face_east
    gain_west = square * face_west
    gain_north = square * face_north
    gain_south = square * face_south
    gain_own = gain_east + gain_west + gain_north + gain_south
    flow_east = wave_gain * face_east * flow_east
    flow_north = wave_gain * face_north * flow_north
    spread = flow_east - west(flow_east) + flow_north - south(flow_north)

    others = pl.ds(1, chips - 1)
    whole = copy_to(
        2, dense.at[others], flux_in.at[others], flux_sems.at[0], flux_sems.at[1]
    )
    whole.wait_recv()

    flux_in[0] = dense[0]
    wide = 8 if chips % 8 == 0 else 1

    def gather(turn, total):
        part = flux_in[pl.ds(turn * wide, wide)].astype(F32)
        return total + jnp.sum(part, axis=0)

    flux = lax.fori_loop(
        0, chips // wide, gather, jnp.zeros((fields * rows, width), F32), unroll=chips <= 32
    )
    heating = flux[0:rows]
    fresh = flux[rows : 2 * rows]
    force_out[pl.ds(0, rows), :] = fresh * wet
    force_out[pl.ds(rows, 2 * rows), :] = flux[2 * rows : 4 * rows]
    forces = []
    for i, offset in enumerate(offsets):
        arrives = offsets.index(-offset)
        forces.append(
            copy_to(
                offset, force_out, force_in.at[arrives], force_send.at[i], force_recv.at[arrives]
            )
        )
    for copy in forces:
        copy.start()

    heat = heating_gain * heating * wet
    for l in range(levels):
        work[l] = work[l] + heat * response[l]
    second_out[0] = work[:, rows - 1, :]
    second_out[1] = work[:, 0, :]
    seconds = [
        copy_to(1, second_out.at[0], second_in.at[0], second_send.at[0], second_recv.at[0]),
        copy_to(-1, second_out.at[1], second_in.at[1], second_send.at[1], second_recv.at[1]),
    ]
    for copy in seconds:
        copy.start()

    for copy in forces:
        copy.wait_recv()
    fresh_tall = fresh_gain * window(force_out, force_in, 0)
    push_east = (wave_gain * stress_gain) * face_east * window(force_out, force_in, rows)
    push_north = (wave_gain * stress_gain) * face_north * window(force_out, force_in, 2 * rows)
    push = push_east - west(push_east) + push_north - south(push_north)

    left = steps
    for stage in range(reach):
        turns = min(rows, left)
        left -= turns

        def subcycle(_, state):
            height, spread = state
            here = (spread + push) + gain_own * height
            sides = gain_east * east(height) + gain_west * west(height)
            ends = gain_north * north(height) + gain_south * south(height)
            spread = here - sides - ends
            return (height + fresh_tall) - spread, spread

        height, spread = lax.fori_loop(0, turns, subcycle, (height, spread), unroll=True)
        trim = lambda v: v[rows:-rows]
        height, spread, push, fresh_tall = map(trim, (height, spread, push, fresh_tall))
        gain_own, gain_east, gain_west, gain_north, gain_south = map(
            trim, (gain_own, gain_east, gain_west, gain_north, gain_south)
        )
    for copy in seconds:
        copy.wait_recv()
    surface = [jnp.zeros((rows, width), F32)] * 4
    for l in range(levels):
        explicit = mixed(work, second_in, l)
        if l == 0:
            explicit = explicit + heat
        out_tracer[l] = explicit
        surface[l % 4] = surface[l % 4] + response[l] * explicit
    surface = (surface[0] + surface[1]) + (surface[2] + surface[3])

    surface_all[0] = jnp.concatenate([surface, height], axis=0).astype(BF16)

    def share(slot, _):
        copy_to(
            slot, surface_all.at[0], surface_all.at[slot], surface_sems.at[0], surface_sems.at[1]
        ).start()
        return 0

    lax.fori_loop(1, count, share, 0)
    out_height[...] = height
    solve(lambda l: out_tracer[l], out_tracer)

    high = 2 * rows
    spot = iota((sources, count * high), 1)
    spot_row = wrapped(me - idiv(spot, high), count) * rows + imod(spot, rows)
    spot_field = idiv(imod(spot, high), rows)
    picks = []
    for k in range(links):
        match = spot_row == target[k]
        for f in range(2):
            picks.append(jnp.where(match & (spot_field == f), 1.0, 0.0))
    out_picks[...] = jnp.concatenate(picks, axis=0).astype(BF16)

    everyone = copy_to(
        1,
        surface_all.at[pl.ds(1, count - 1)],
        surface_all.at[pl.ds(1, count - 1)],
        surface_sems.at[0],
        surface_sems.at[1],
    )
    everyone.wait_recv()
    for copy in edges + bases + forces + seconds:
        copy.wait_send()
    whole.wait_send()
    for c in range(chunks):
        swap(c).wait_send()
    everyone.wait_send()


def finish(
    tracer_ref,
    height_ref,
    weight_ref,
    surface_ref,
    picks_ref,
    out_tracer,
    out_height,
    out_air,
    returned,
    sems,
):
    sources, links, cols, width = weight_ref.shape[1:]
    pair = 2 if sources % 2 == 0 else 1
    stores = [
        pltpu.make_async_copy(tracer_ref, out_tracer, sems.at[0]),
        pltpu.make_async_copy(height_ref, out_height, sems.at[1]),
    ]
    for copy in stores:
        copy.start()
    chosen = jnp.dot(
        picks_ref[...], surface_ref[...].reshape(-1, width), preferred_element_type=F32
    ).astype(BF16)
    both = 2 * sources
    chosen = jnp.concatenate([chosen[k * both : (k + 1) * both] for k in range(links)], axis=1)
    results = []
    for p in range(sources // pair):
        rhs = jnp.concatenate(
            [
                weight_ref[0, pl.ds(p * pair, pair), k].reshape(pair * cols, width)
                for k in range(links)
            ],
            axis=1,
        )
        full = lax.dot_general(
            chosen, rhs, (((1,), (1,)), ((), ())), preferred_element_type=F32
        ).reshape(2, sources, pair * cols)
        belongs = iota(full.shape, 1) == p * pair + idiv(iota(full.shape, 2), cols)
        results.append(jnp.sum(jnp.where(belongs, full, 0.0), axis=1))
    returned[0] = jnp.concatenate(results, axis=1).astype(BF16)
    last = pltpu.make_async_copy(returned, out_air, sems.at[2])
    last.start()
    for copy in stores + [last]:
        copy.wait()


def shards(count, blocks_dom, air, weights, targets, tracer, mix, height, flow, wet):
    fields = air.shape[1]
    sources, links = weights.shape[1:3]
    levels, rows, width = tracer.shape
    sides = 2 * -(-NSTEP * NSUB // rows)
    column = pltpu.VMEM((levels, rows, width), F32)
    spec = pl.BlockSpec(memory_space=pltpu.VMEM)
    dma = pltpu.SemaphoreType.DMA
    space = pl.BlockSpec(memory_space=pltpu.HBM)
    out_air = jax.ShapeDtypeStruct((1, 2, air.shape[2]), BF16)
    out_tracer = jax.ShapeDtypeStruct(tracer.shape, F32)
    out_height = jax.ShapeDtypeStruct(height.shape, F32)
    operands = (air, weights, jnp.swapaxes(targets, 1, 2), tracer, mix, height, flow, wet)
    operands = [pltpu.with_memory_space_constraint(v, pltpu.HBM) for v in operands]
    parts = pl.pallas_call(
        functools.partial(kernel, count, blocks_dom),
        out_shape=(
            out_tracer,
            out_height,
            jax.ShapeDtypeStruct(weights.shape, BF16),
            jax.ShapeDtypeStruct((count, 2 * rows, width), BF16),
            jax.ShapeDtypeStruct((2 * sources * links, count * 2 * rows), BF16),
        ),
        in_specs=[space] * 8,
        out_specs=(spec,) * 5,
        scratch_shapes=[
            pltpu.VMEM(air.shape, BF16),
            pltpu.VMEM((1, links, sources), jnp.int32),
            pltpu.VMEM(tracer.shape, F32),
            pltpu.VMEM(mix.shape, F32),
            pltpu.VMEM(wet.shape, jnp.int32),
            pltpu.VMEM((sources * links * fields, width), F32),
            *[pltpu.VMEM((count // 2, fields * rows, width), BF16)] * 4,
            pltpu.VMEM((4 * rows, width), F32),
            pltpu.VMEM((sides, 4 * rows, width), F32),
            pltpu.VMEM((2, levels + rows, width), F32),
            pltpu.VMEM((2, levels + rows, width), F32),
            pltpu.VMEM((3 * rows, width), F32),
            pltpu.VMEM((sides, 3 * rows, width), F32),
            pltpu.VMEM((2, levels, width), F32),
            pltpu.VMEM((2, levels, width), F32),
            column,
            column,
            column,
            column,
            column,
            dma((8,)),
            dma((sources,)),
            dma((2, count // 2)),
            dma((2,)),
            dma((sides,)),
            dma((sides,)),
            dma((2,)),
            dma((2,)),
            dma((sides,)),
            dma((sides,)),
            dma((2,)),
            dma((2,)),
            dma((2,)),
        ],
        compiler_params=pltpu.CompilerParams(
            collective_id=0, has_side_effects=True, vmem_limit_bytes=32 * 1024 * 1024
        ),
    )(*operands)
    return pl.pallas_call(
        finish,
        out_shape=(out_tracer, out_height, out_air),
        in_specs=[spec] * 5,
        out_specs=(space,) * 3,
        scratch_shapes=[pltpu.VMEM(out_air.shape, BF16), dma((3,))],
        compiler_params=pltpu.CompilerParams(vmem_limit_bytes=32 * 1024 * 1024),
    )(*parts)


def solution(mesh):
    count = mesh.shape["comp"] * mesh.shape["dom"]
    return jax.shard_map(
        functools.partial(shards, count, mesh.shape["dom"]),
        mesh=mesh,
        in_specs=(
            P("comp", None, "dom"),
            P("comp", "dom", None, None, None),
            P("comp", "dom", None),
            P(None, ("comp", "dom"), None),
            P(None, ("comp", "dom"), None),
            P(("comp", "dom"), None),
            P(None, ("comp", "dom"), None),
            P(("comp", "dom"), None),
        ),
        out_specs=(
            P(None, ("comp", "dom"), None),
            P(("comp", "dom"), None),
            P("comp", None, "dom"),
        ),
        check_vma=False,
    )
```

```python
import functools

import jax
import jax.numpy as jnp
from jax import lax
from jax.experimental import pallas as pl
from jax.experimental.pallas import tpu as pltpu
from jax.sharding import PartitionSpec as P

NSTEP = 2
NSUB = 8

wave_gain = 0.35
stress_gain = 0.1
fresh_gain = 0.1
spread_gain = 0.2
heating_gain = 0.5

MESH = pl.DeviceIdType.MESH
F32 = jnp.float32
BF16 = jnp.bfloat16


def idiv(value, by):
    if by & (by - 1) == 0:
        return lax.shift_right_logical(value, jnp.full_like(value, by.bit_length() - 1))
    return value // by


def imod(value, by):
    if by & (by - 1) == 0:
        return value & (by - 1)
    return value % by


def wrapped(value, count):
    value = jnp.where(value >= count, value - count, value)
    return jnp.where(value < 0, value + count, value)


def iota(shape, dim):
    return lax.broadcasted_iota(jnp.int32, shape, dim)


def east(v):
    return pltpu.roll(v, v.shape[-1] - 1, v.ndim - 1)


def west(v):
    return pltpu.roll(v, 1, v.ndim - 1)


def north(v):
    return pltpu.roll(v, v.shape[-2] - 1, v.ndim - 2)


def south(v):
    return pltpu.roll(v, 1, v.ndim - 2)


def kernel(
    count,
    blocks_dom,
    air_hbm,
    weight_hbm,
    target_hbm,
    tracer_hbm,
    mix_hbm,
    height_hbm,
    flow_hbm,
    wet_hbm,
    out_tracer,
    out_height,
    weight_ref,
    surface_all,
    out_picks,
    air_ref,
    target_ref,
    tracer_ref,
    mix_ref,
    wet_ref,
    terms,
    swap_out,
    swap_in,
    dense,
    flux_in,
    base_out,
    base_in,
    edge_out,
    edge_in,
    force_out,
    force_in,
    second_out,
    second_in,
    inverse,
    carry,
    ratio,
    response,
    work,
    load_sems,
    weight_sems,
    swap_sems,
    flux_sems,
    base_send,
    base_recv,
    edge_send,
    edge_recv,
    force_send,
    force_recv,
    second_send,
    second_recv,
    surface_sems,
):
    group, block = lax.axis_index("comp"), lax.axis_index("dom")
    me = group * blocks_dom + block
    fields = air_ref.shape[1]
    sources, links, cols, width = weight_ref.shape[1:]
    levels, rows = tracer_ref.shape[:2]
    steps = NSTEP * NSUB
    reach = -(-steps // rows)
    offsets = [d for d in range(-reach, reach + 1) if d != 0]
    pair = 2 if sources % 2 == 0 else 1

    def device(offset):
        peer = lax.rem(me + offset + count, count)
        return (peer // blocks_dom, lax.rem(peer, blocks_dom))

    def copy_to(offset, src, dst, send, recv):
        return pltpu.make_async_remote_copy(
            src_ref=src,
            dst_ref=dst,
            send_sem=send,
            recv_sem=recv,
            device_id=device(offset),
            device_id_type=MESH,
        )

    pairs = sources // pair
    weight_loads = [
        pltpu.make_async_copy(
            weight_hbm.at[:, pl.ds(p * pair, pair)],
            weight_ref.at[:, pl.ds(p * pair, pair)],
            weight_sems.at[p],
        )
        for p in range(pairs)
    ]
    loads = [
        pltpu.make_async_copy(src, dst, load_sems.at[i])
        for i, (src, dst) in enumerate(
            [
                (air_hbm, air_ref),
                (target_hbm, target_ref),
                (wet_hbm, wet_ref),
                (tracer_hbm, tracer_ref),
                (height_hbm, base_out.at[pl.ds(0, rows)]),
                (flow_hbm.at[0], base_out.at[pl.ds(rows, rows)]),
                (flow_hbm.at[1], base_out.at[pl.ds(2 * rows, rows)]),
                (mix_hbm, mix_ref),
            ]
        )
    ]
    for copy in loads[:2] + weight_loads + loads[2:]:
        copy.start()

    barrier = pltpu.get_barrier_semaphore()

    def greet(offset, _):
        pl.semaphore_signal(barrier, inc=1, device_id=device(offset), device_id_type=MESH)
        return 0

    lax.fori_loop(1, count, greet, 0)

    loads[0].wait()
    loads[1].wait()
    exchange = air_ref[0].astype(F32)
    group_rows = pair * fields
    own = idiv(iota((group_rows, pair * cols), 0), fields) == idiv(
        iota((group_rows, pair * cols), 1), cols
    )
    for p in range(pairs):
        weight_loads[p].wait()
        part = exchange[:, p * pair * cols : (p + 1) * pair * cols]
        lhs = jnp.where(own, jnp.concatenate([part] * pair, axis=0), 0.0).astype(BF16)
        for k in range(links):
            rhs = weight_ref[0, pl.ds(p * pair, pair), k].reshape(pair * cols, width)
            terms[pl.ds((p * links + k) * group_rows, group_rows), :] = jnp.dot(
                lhs, rhs, preferred_element_type=F32
            )
    every = sources * links * fields
    diagonal = iota((sources, sources), 0) == iota((sources, sources), 1)
    numbers = target_ref[0].astype(F32)
    target = [
        jnp.sum(jnp.where(diagonal, numbers[k : k + 1], 0.0), axis=1, keepdims=True).astype(
            jnp.int32
        )
        for k in range(links)
    ]
    lane = iota((sources, every), 1)
    lane_field = imod(lane, fields)
    lane_source = idiv(lane, group_rows * links) * pair + imod(idiv(lane, fields), pair)
    lane_link = imod(idiv(lane, group_rows), links)
    here = lane_source == iota((sources, every), 0)
    lane_target = jnp.zeros((sources, every), jnp.int32)
    for k in range(links):
        lane_target = jnp.where(here & (lane_link == k), target[k], lane_target)
    lane_target = jnp.sum(lane_target, axis=0, keepdims=True)
    lane_key = lane_target * fields + lane_field[:1]
    value = terms[...]
    upper = value.astype(BF16)
    lower = (value - upper.astype(F32)).astype(BF16)
    split = jnp.concatenate([upper, lower], axis=0)

    for copy in loads[2:4]:
        copy.wait()
    wet = wet_ref[...].astype(F32)
    base_out[pl.ds(3 * rows, rows), :] = wet
    edge_out[0, pl.ds(0, levels), :] = tracer_ref[:, rows - 1, :]
    edge_out[1, pl.ds(0, levels), :] = tracer_ref[:, 0, :]
    edge_out[0, pl.ds(levels, rows), :] = wet
    edge_out[1, pl.ds(levels, rows), :] = wet

    pl.semaphore_wait(barrier, count - 1)

    edges = [
        copy_to(1, edge_out.at[0], edge_in.at[0], edge_send.at[0], edge_recv.at[0]),
        copy_to(-1, edge_out.at[1], edge_in.at[1], edge_send.at[1], edge_recv.at[1]),
    ]
    for copy in edges:
        copy.start()

    chips = count // 2
    chip, core = me // 2, lax.rem(me, 2)
    sibling = 1 - 2 * core
    chunk = 8 if chips % 8 == 0 else 1
    chunks = chips // chunk
    shape = (chunk, fields, rows, every)

    def placed(c, place):
        to_chip = wrapped(iota(shape, 0) + (c * chunk + chip), chips)
        row_key = ((to_chip * 2 + place) * rows + iota(shape, 2)) * fields + iota(shape, 1)
        row_key = row_key.reshape(chunk * fields * rows, every)
        hot = jnp.where(row_key == lane_key, 1.0, 0.0).astype(BF16)
        hot = jnp.concatenate([hot, hot], axis=1)
        result = jnp.dot(hot, split, preferred_element_type=F32)
        return result.reshape(chunk, fields * rows, width)

    def swap(c):
        part = pl.ds(c * chunk, chunk)
        return copy_to(
            sibling, swap_out.at[part], swap_in.at[part], swap_sems.at[0, c], swap_sems.at[1, c]
        )

    def give(turn, _):
        c = lax.rem(turn + 1, chunks)
        swap_out[pl.ds(c * chunk, chunk)] = placed(c, 1 - core).astype(BF16)
        swap(c).start()
        return 0

    lax.fori_loop(0, chunks, give, 0)

    def keep(turn, _):
        c = lax.rem(turn + 1, chunks)
        part = pl.ds(c * chunk, chunk)
        mine = placed(c, core)
        swap(c).wait_recv()
        dense[part] = (mine + swap_in[part].astype(F32)).astype(BF16)

        def send(b, _):
            slot = c * chunk + b

            @pl.when(slot > 0)
            def _():
                copy_to(
                    2 * slot,
                    dense.at[slot],
                    flux_in.at[slot],
                    flux_sems.at[0],
                    flux_sems.at[1],
                ).start()

            return 0

        lax.fori_loop(0, chunk, send, 0)
        return 0

    lax.fori_loop(0, chunks, keep, 0)

    for copy in loads[4:]:
        copy.wait()
    bases = []
    for i, offset in enumerate(offsets):
        arrives = offsets.index(-offset)
        bases.append(
            copy_to(offset, base_out, base_in.at[arrives], base_send.at[i], base_recv.at[arrives])
        )
    for copy in bases:
        copy.start()

    zero = jnp.zeros((rows, width), F32)
    last_ratio = None
    last_response = None
    for l in range(levels):
        up = mix_ref[l - 1] if l > 0 else zero
        down = mix_ref[l] if l < levels - 1 else zero
        pivot = 1.0 + up + down
        if l > 0:
            pivot = pivot - up * last_ratio
        inv = 1.0 / pivot
        inverse[l] = inv
        carry[l] = up * inv
        last_response = inv if l == 0 else up * inv * last_response
        response[l] = last_response
        last_ratio = down * inv
        ratio[l] = last_ratio
    for l in range(levels - 2, -1, -1):
        last_response = response[l] + ratio[l] * last_response
        response[l] = last_response

    for copy in edges:
        copy.wait_recv()
    row = iota((rows, width), 0)
    top = row == rows - 1
    bottom = row == 0
    wet_north = jnp.where(top, edge_in[1, pl.ds(levels, 1), :], north(wet))
    wet_south = jnp.where(bottom, edge_in[0, pl.ds(levels + rows - 1, 1), :], south(wet))
    inside_top = jnp.logical_not(top & (me == count - 1))
    inside_bottom = jnp.logical_not(bottom & (me == 0))
    mix_east = spread_gain * wet * east(wet)
    mix_west = spread_gain * wet * west(wet)
    mix_north = jnp.where(inside_top, spread_gain * wet * wet_north, 0.0)
    mix_south = jnp.where(inside_bottom, spread_gain * wet * wet_south, 0.0)
    mix_own = 1.0 - (mix_east + mix_west + mix_north + mix_south)

    def mixed(source, halo, l):
        v = source[l]
        v_north = jnp.where(top, halo[1, pl.ds(l, 1), :], north(v))
        v_south = jnp.where(bottom, halo[0, pl.ds(l, 1), :], south(v))
        return (
            (mix_own * v + mix_east * east(v))
            + mix_west * west(v)
            + (mix_north * v_north + mix_south * v_south)
        )

    def solve(explicit, result):
        swept = None
        for l in range(levels):
            swept = explicit(l) * inverse[l] if l == 0 else explicit(l) * inverse[l] + carry[l] * swept
            result[l] = swept
        for l in range(levels - 2, -1, -1):
            swept = result[l] + ratio[l] * swept
            result[l] = swept

    solve(lambda l: mixed(tracer_ref, edge_in, l), work)

    for copy in bases:
        copy.wait_recv()

    def window(own_ref, arrived, start):
        parts = []
        for offset in range(-reach, reach + 1):
            if offset == 0:
                parts.append(own_ref[pl.ds(start, rows), :])
            else:
                parts.append(arrived[offsets.index(offset), pl.ds(start, rows), :])
        return jnp.concatenate(parts, axis=0)

    tall = (2 * reach + 1) * rows
    height = window(base_out, base_in, 0)
    flow_east = window(base_out, base_in, rows)
    flow_north = window(base_out, base_in, 2 * rows)
    wet_tall = window(base_out, base_in, 3 * rows)
    number = wrapped(me * rows - reach * rows + iota((tall, width), 0), count * rows)
    face_east = wet_tall * east(wet_tall)
    face_north = jnp.where(number == count * rows - 1, 0.0, wet_tall * north(wet_tall))
    face_west = west(face_east)
    face_south = south(face_north)
    square = wave_gain * wave_gain
    gain_east = square * face_east
    gain_west = square * face_west
    gain_north = square * face_north
    gain_south = square * face_south
    gain_own = gain_east + gain_west + gain_north + gain_south
    flow_east = wave_gain * face_east * flow_east
    flow_north = wave_gain * face_north * flow_north
    spread = flow_east - west(flow_east) + flow_north - south(flow_north)

    others = pl.ds(1, chips - 1)
    whole = copy_to(
        2, dense.at[others], flux_in.at[others], flux_sems.at[0], flux_sems.at[1]
    )
    whole.wait_recv()

    flux_in[0] = dense[0]
    wide = 8 if chips % 8 == 0 else 1

    def gather(turn, total):
        part = flux_in[pl.ds(turn * wide, wide)].astype(F32)
        return total + jnp.sum(part, axis=0)

    flux = lax.fori_loop(
        0, chips // wide, gather, jnp.zeros((fields * rows, width), F32), unroll=chips <= 32
    )
    heating = flux[0:rows]
    fresh = flux[rows : 2 * rows]
    force_out[pl.ds(0, rows), :] = fresh * wet
    force_out[pl.ds(rows, 2 * rows), :] = flux[2 * rows : 4 * rows]
    forces = []
    for i, offset in enumerate(offsets):
        arrives = offsets.index(-offset)
        forces.append(
            copy_to(
                offset, force_out, force_in.at[arrives], force_send.at[i], force_recv.at[arrives]
            )
        )
    for copy in forces:
        copy.start()

    heat = heating_gain * heating * wet
    for l in range(levels):
        work[l] = work[l] + heat * response[l]
    second_out[0] = work[:, rows - 1, :]
    second_out[1] = work[:, 0, :]
    seconds = [
        copy_to(1, second_out.at[0], second_in.at[0], second_send.at[0], second_recv.at[0]),
        copy_to(-1, second_out.at[1], second_in.at[1], second_send.at[1], second_recv.at[1]),
    ]
    for copy in seconds:
        copy.start()

    for copy in forces:
        copy.wait_recv()
    fresh_tall = fresh_gain * window(force_out, force_in, 0)
    push_east = (wave_gain * stress_gain) * face_east * window(force_out, force_in, rows)
    push_north = (wave_gain * stress_gain) * face_north * window(force_out, force_in, 2 * rows)
    push = push_east - west(push_east) + push_north - south(push_north)

    left = steps
    for stage in range(reach):
        if stage == reach - 1:
            for copy in seconds:
                copy.wait_recv()
            surface = [jnp.zeros((rows, width), F32)] * 4
            for l in range(levels):
                explicit = mixed(work, second_in, l)
                if l == 0:
                    explicit = explicit + heat
                out_tracer[l] = explicit
                surface[l % 4] = surface[l % 4] + response[l] * explicit
            surface = (surface[0] + surface[1]) + (surface[2] + surface[3])
        turns = min(rows, left)
        left -= turns

        def subcycle(_, state):
            height, spread = state
            here = (spread + push) + gain_own * height
            sides = gain_east * east(height) + gain_west * west(height)
            ends = gain_north * north(height) + gain_south * south(height)
            spread = here - sides - ends
            return (height + fresh_tall) - spread, spread

        height, spread = lax.fori_loop(0, turns, subcycle, (height, spread), unroll=True)
        trim = lambda v: v[rows:-rows]
        height, spread, push, fresh_tall = map(trim, (height, spread, push, fresh_tall))
        gain_own, gain_east, gain_west, gain_north, gain_south = map(
            trim, (gain_own, gain_east, gain_west, gain_north, gain_south)
        )
    surface_all[0] = jnp.concatenate([surface, height], axis=0).astype(BF16)

    def share(turn, _):
        slot = 1 + lax.rem(turn + blocks_dom - 1, count - 1)
        copy_to(
            slot, surface_all.at[0], surface_all.at[slot], surface_sems.at[0], surface_sems.at[1]
        ).start()
        return 0

    lax.fori_loop(0, count - 1, share, 0)
    out_height[...] = height
    solve(lambda l: out_tracer[l], out_tracer)

    high = 2 * rows
    spot = iota((sources, count * high), 1)
    spot_row = wrapped(me - idiv(spot, high), count) * rows + imod(spot, rows)
    spot_field = idiv(imod(spot, high), rows)
    picks = []
    for k in range(links):
        match = spot_row == target[k]
        for f in range(2):
            picks.append(jnp.where(match & (spot_field == f), 1.0, 0.0))
    out_picks[...] = jnp.concatenate(picks, axis=0).astype(BF16)

    everyone = copy_to(
        1,
        surface_all.at[pl.ds(1, count - 1)],
        surface_all.at[pl.ds(1, count - 1)],
        surface_sems.at[0],
        surface_sems.at[1],
    )
    everyone.wait_recv()
    for copy in edges + bases + forces + seconds:
        copy.wait_send()
    whole.wait_send()
    for c in range(chunks):
        swap(c).wait_send()
    everyone.wait_send()


def finish(
    tracer_ref,
    height_ref,
    weight_ref,
    surface_ref,
    picks_ref,
    out_tracer,
    out_height,
    out_air,
    returned,
    sems,
):
    sources, links, cols, width = weight_ref.shape[1:]
    pair = 2 if sources % 2 == 0 else 1
    stores = [
        pltpu.make_async_copy(tracer_ref, out_tracer, sems.at[0]),
        pltpu.make_async_copy(height_ref, out_height, sems.at[1]),
    ]
    for copy in stores:
        copy.start()
    chosen = jnp.dot(
        picks_ref[...], surface_ref[...].reshape(-1, width), preferred_element_type=F32
    ).astype(BF16)
    both = 2 * sources
    chosen = jnp.concatenate([chosen[k * both : (k + 1) * both] for k in range(links)], axis=1)
    results = []
    for p in range(sources // pair):
        rhs = jnp.concatenate(
            [
                weight_ref[0, pl.ds(p * pair, pair), k].reshape(pair * cols, width)
                for k in range(links)
            ],
            axis=1,
        )
        full = lax.dot_general(
            chosen, rhs, (((1,), (1,)), ((), ())), preferred_element_type=F32
        ).reshape(2, sources, pair * cols)
        belongs = iota(full.shape, 1) == p * pair + idiv(iota(full.shape, 2), cols)
        results.append(jnp.sum(jnp.where(belongs, full, 0.0), axis=1))
    returned[0] = jnp.concatenate(results, axis=1).astype(BF16)
    last = pltpu.make_async_copy(returned, out_air, sems.at[2])
    last.start()
    for copy in stores + [last]:
        copy.wait()


def shards(count, blocks_dom, air, weights, targets, tracer, mix, height, flow, wet):
    fields = air.shape[1]
    sources, links = weights.shape[1:3]
    levels, rows, width = tracer.shape
    sides = 2 * -(-NSTEP * NSUB // rows)
    column = pltpu.VMEM((levels, rows, width), F32)
    spec = pl.BlockSpec(memory_space=pltpu.VMEM)
    dma = pltpu.SemaphoreType.DMA
    space = pl.BlockSpec(memory_space=pltpu.HBM)
    out_air = jax.ShapeDtypeStruct((1, 2, air.shape[2]), BF16)
    out_tracer = jax.ShapeDtypeStruct(tracer.shape, F32)
    out_height = jax.ShapeDtypeStruct(height.shape, F32)
    operands = (air, weights, jnp.swapaxes(targets, 1, 2), tracer, mix, height, flow, wet)
    operands = [pltpu.with_memory_space_constraint(v, pltpu.HBM) for v in operands]
    parts = pl.pallas_call(
        functools.partial(kernel, count, blocks_dom),
        out_shape=(
            out_tracer,
            out_height,
            jax.ShapeDtypeStruct(weights.shape, BF16),
            jax.ShapeDtypeStruct((count, 2 * rows, width), BF16),
            jax.ShapeDtypeStruct((2 * sources * links, count * 2 * rows), BF16),
        ),
        in_specs=[space] * 8,
        out_specs=(spec,) * 5,
        scratch_shapes=[
            pltpu.VMEM(air.shape, BF16),
            pltpu.VMEM((1, links, sources), jnp.int32),
            pltpu.VMEM(tracer.shape, F32),
            pltpu.VMEM(mix.shape, F32),
            pltpu.VMEM(wet.shape, jnp.int32),
            pltpu.VMEM((sources * links * fields, width), F32),
            *[pltpu.VMEM((count // 2, fields * rows, width), BF16)] * 4,
            pltpu.VMEM((4 * rows, width), F32),
            pltpu.VMEM((sides, 4 * rows, width), F32),
            pltpu.VMEM((2, levels + rows, width), F32),
            pltpu.VMEM((2, levels + rows, width), F32),
            pltpu.VMEM((3 * rows, width), F32),
            pltpu.VMEM((sides, 3 * rows, width), F32),
            pltpu.VMEM((2, levels, width), F32),
            pltpu.VMEM((2, levels, width), F32),
            column,
            column,
            column,
            column,
            column,
            dma((8,)),
            dma((sources,)),
            dma((2, count // 2)),
            dma((2,)),
            dma((sides,)),
            dma((sides,)),
            dma((2,)),
            dma((2,)),
            dma((sides,)),
            dma((sides,)),
            dma((2,)),
            dma((2,)),
            dma((2,)),
        ],
        compiler_params=pltpu.CompilerParams(
            collective_id=0, has_side_effects=True, vmem_limit_bytes=32 * 1024 * 1024
        ),
    )(*operands)
    return pl.pallas_call(
        finish,
        out_shape=(out_tracer, out_height, out_air),
        in_specs=[spec] * 5,
        out_specs=(space,) * 3,
        scratch_shapes=[pltpu.VMEM(out_air.shape, BF16), dma((3,))],
        compiler_params=pltpu.CompilerParams(vmem_limit_bytes=32 * 1024 * 1024),
    )(*parts)


def solution(mesh):
    count = mesh.shape["comp"] * mesh.shape["dom"]
    return jax.shard_map(
        functools.partial(shards, count, mesh.shape["dom"]),
        mesh=mesh,
        in_specs=(
            P("comp", None, "dom"),
            P("comp", "dom", None, None, None),
            P("comp", "dom", None),
            P(None, ("comp", "dom"), None),
            P(None, ("comp", "dom"), None),
            P(("comp", "dom"), None),
            P(None, ("comp", "dom"), None),
            P(("comp", "dom"), None),
        ),
        out_specs=(
            P(None, ("comp", "dom"), None),
            P(("comp", "dom"), None),
            P("comp", None, "dom"),
        ),
        check_vma=False,
    )
```
